32 devices in a mesh: group: 8 (over z, y), local: 4 (over x, core).
Axes of the slice: x: 2, y: 2, z: 4, core: 2. Of those that a mesh axis runs over, the one named last changes fastest.
Arguments:
- inputs: bfloat16 [16384, 768], P(('group', 'local')), may hold values from -6 to 6
- segments: int32 [32, 512], P(('group', 'local')), may hold values from 0 to 7, never falling along the last dimension, each value on 1 to 256 neighbouring positions
- expert_index: int32 [16384, 1], P(('group', 'local')), may hold values from 0 to 31
- gain_attn: float32 [768], replicated, may hold values from 0.5 to 1.5
- query_weight: bfloat16 [768, 768], replicated, may hold values from -0.21875 to 0.21875
- key_weight: bfloat16 [768, 768], replicated, may hold values from -0.21875 to 0.21875
- value_weight: bfloat16 [768, 768], replicated, may hold values from -0.21875 to 0.21875
- output_weight: bfloat16 [768, 768], replicated, may hold values from -0.875 to 0.875
- bias_table: float32 [32, 12], replicated, may hold values from -4 to 4
- gain_ffn: float32 [768], replicated, may hold values from 0.5 to 1.5
- router_weight: bfloat16 [768, 32], replicated, may hold values from -0.21875 to 0.21875
- expert_in: bfloat16 [32, 768, 3072], P(('group', 'local')), may hold values from -0.21875 to 0.21875
- expert_out: bfloat16 [32, 3072, 768], P(('group', 'local')), may hold values from -4 to 4, as said below
- cotangent: bfloat16 [16384, 768], P(('group', 'local')), may hold values from -6 to 6
Outputs:
- output: bfloat16 [16384, 768], P(('group', 'local'))
- input_grad: bfloat16 [16384, 768], P(('group', 'local'))
- gain_attn_grad: float32 [768], replicated
- query_grad: float32 [768, 768], replicated
- key_grad: float32 [768, 768], replicated
- value_grad: float32 [768, 768], replicated
- output_weight_grad: float32 [768, 768], replicated
- bias_table_grad: float32 [32, 12], replicated
- gain_ffn_grad: float32 [768], replicated
- router_grad: float32 [768, 32], replicated
- expert_in_grad: float32 [32, 768, 3072], P(('group', 'local'))
- expert_out_grad: float32 [32, 3072, 768], P(('group', 'local'))
- expert_counts: int32 [2, 32], replicated
The draws below stay inside these ranges and needn't reach their ends.
Inputs may be any that keep to these rules, and one draw needn't show every extreme that they name: `expert_out`: entries of mean zero and deviation 32 / sqrt(3072).
All inputs are finite; a program needn't handle non-finite values.
Results may differ from the reference program's by a relative error of at most 0.015.
Values may be sent and summed in bfloat16 or wider, within the bound.
A program may use at most 192 MiB of HBM per device.

```python
import math
from functools import partial
import jax
import jax.numpy as jnp
import numpy as np
from jax import lax

D = 768
H = 12
HD = 64
FF = 3072
NB = 32
SEQ = 512
DOCS = 8
TOK_DEV = 512
EXPERTS = 32
TOKENS = 16384
SEQS = 32
CAP = 20
SLOTS = 640
N_GROUP = 8
N_LOCAL = 4


def draw_expert_out(key, part):
    key = jax.random.fold_in(key, 7)
    spread = EXPERTS / math.sqrt(FF)
    sample = jax.random.truncated_normal(key, -4.0, 4.0, (EXPERTS, FF, D), jnp.float32)
    limit_value = float(EXPERTS // 8)
    return jnp.clip(sample * spread, -limit_value, limit_value).astype(jnp.bfloat16)


def block_scale(own_key, extent, cuts, least, high):
    loudness = 1.0
    for dim, shards_of in cuts:
        heights = jax.random.uniform(jax.random.fold_in(jax.random.fold_in(own_key, 6), dim), (shards_of,), jnp.float32, least / len(cuts), high / len(cuts))
        loudness = loudness * jnp.repeat(jnp.exp(heights), extent[dim] // shards_of).reshape((-1,) + (1,) * (len(extent) - 1 - dim))
    return loudness


def distinct(stream_key, rows, number_of, top, lift):
    sequence = jax.random.permutation(jax.random.fold_in(stream_key, 1), number_of)
    boost = sequence
    for power in range(3):
        boost = boost * boost // number_of
    boost = boost * lift // number_of
    chance = jax.random.randint(jax.random.fold_in(stream_key, 2), (rows, number_of), 0, 4096) + boost
    sure = jax.random.permutation(jax.random.fold_in(stream_key, 3), rows)[jnp.arange(number_of) % rows]
    chance = jnp.where(jnp.arange(rows)[:, None] == sure[None, :], 1 << 14, chance)
    priority = chance * number_of + jnp.arange(number_of)
    return lax.top_k(priority.astype(jnp.int32), top)[1].astype(jnp.int32)


def split_up(count, total, limit, slope):
    loads = [(1 << 20) // math.isqrt(standing ** slope) + 1 for standing in range(2, count + 1)]
    surplus, holding = total - limit - (count - 1), [1] * (count - 1)
    while surplus > 0:
        free = [i for i in range(count - 1) if holding[i] < limit]
        pool, budget = sum([loads[i] for i in free]), surplus
        for i in free:
            more = min(limit - holding[i], max(1, budget * loads[i] // pool), surplus)
            holding[i] = holding[i] + more
            surplus = surplus - more
    return np.array([limit] + holding)


def uneven_parts(key, count, total, limit, lean):
    if count == 2:
        one = jax.random.randint(key, (), max(1, total - limit), min(limit, total - 1) + 1)
        return jnp.stack([one, total - one])
    lengths = jnp.asarray(split_up(count, total, limit, lean), jnp.int32)
    twos = (count - 1) // 2
    giver, receiver = lengths[1:1 + 2 * twos:2], lengths[2:2 + 2 * twos:2]
    slack = jnp.minimum(giver - 1, limit - receiver)
    moved = jax.random.randint(jax.random.fold_in(key, 1), (twos,), 0, 1 << 20) % (slack + 1)
    lengths = lengths.at[1:1 + 2 * twos:2].set(giver - moved).at[2:2 + 2 * twos:2].set(receiver + moved)
    return lengths[jax.random.permutation(jax.random.fold_in(key, 2), count)]


def scatter_about(key, dims, deviation, bound, cuts=(), held_as=jnp.bfloat16):
    level = block_scale(key, dims, cuts, -0.22, 0.18) if cuts else 1.0
    drawn = jax.random.normal(key, dims, jnp.float32) * deviation * level
    return jnp.minimum(jnp.maximum(drawn, -bound), bound).astype(held_as)


def setup_inputs(seed: int = 0) -> dict:
    key_of = jax.random.split(jax.random.key(seed), 15)
    inputs = scatter_about(key_of[0], (TOKENS, D), 1.0, 6.0, ((0, 32),))
    segments = jax.vmap(lambda own: jnp.searchsorted(jnp.cumsum(uneven_parts(own, DOCS, SEQ, SEQ // 2, 1)), jnp.arange(SEQ), side="right"))(jax.random.split(key_of[1], SEQS)).reshape((SEQS, SEQ)).astype(jnp.int32)
    expert_index = distinct(key_of[2], TOKENS, EXPERTS, 1, 256)
    gain_attn = jnp.clip(1.0 + 0.1 * jax.random.normal(key_of[3], (D,), jnp.float32), 0.5, 1.5)
    query_weight = scatter_about(key_of[4], (D, D), D ** -0.5, 0.21875)
    key_weight = scatter_about(key_of[5], (D, D), D ** -0.5, 0.21875)
    value_weight = scatter_about(key_of[6], (D, D), D ** -0.5, 0.21875)
    output_weight = scatter_about(key_of[7], (D, D), (D // 16) ** -0.5, 0.875)
    bias_table = scatter_about(key_of[8], (NB, H), 1.0, 4.0, (), jnp.float32)
    gain_ffn = jnp.clip(1.0 + 0.1 * jax.random.normal(key_of[9], (D,), jnp.float32), 0.5, 1.5)
    router_weight = scatter_about(key_of[10], (D, EXPERTS), D ** -0.5, 0.21875)
    expert_in = scatter_about(key_of[11], (EXPERTS, D, FF), D ** -0.5, 0.21875, ((0, 32),))
    expert_out = draw_expert_out(jax.random.fold_in(key_of[14], 71), 0)
    cotangent = scatter_about(key_of[13], (TOKENS, D), 1.0, 6.0, ((0, 32),))
    return dict(inputs=inputs, segments=segments, expert_index=expert_index, gain_attn=gain_attn, query_weight=query_weight, key_weight=key_weight, value_weight=value_weight, output_weight=output_weight, bias_table=bias_table, gain_ffn=gain_ffn, router_weight=router_weight, expert_in=expert_in, expert_out=expert_out, cotangent=cotangent)


@jax.custom_vjp
def low(v):
    return lax.optimization_barrier(v.astype(jnp.bfloat16)).astype(jnp.float32)

@jax.custom_vjp
def low_back(v):
    return v

def low_keep(v):
    return (low(v), None)

def low_pass(kept, grad):
    return (grad,)

def back_keep(v):
    return (v, None)

def back_low(kept, grad):
    return (low(grad),)
low.defvjp(low_keep, low_pass)
low_back.defvjp(back_keep, back_low)
epsilon = 1e-06
score_scale = 0.125
masked_score = -1000000000.0
highest = lax.Precision.HIGHEST
far_limits = (12, 16, 23, 32, 46, 64, 91)

def low_both(value):
    return low(low_back(value))

def rms_scale(values, gain_row):
    return values * lax.rsqrt(lax.optimization_barrier(jnp.mean(values * values, axis=-1, keepdims=True)) + epsilon) * gain_row

def bucket_table(length):
    places = jnp.arange(length, dtype=jnp.int32)
    offset = places[None, :] - places[:, None]
    distance = jnp.abs(offset)
    far_part = jnp.zeros_like(distance) + 8
    for threshold in far_limits:
        far_part = far_part + (distance >= threshold).astype(jnp.int32)
    bucket_near = jnp.where(distance < 8, distance, far_part)
    return bucket_near + 16 * (offset > 0).astype(jnp.int32)

def position_bias(bias_table, length):
    buckets = bucket_table(length)
    picker = (buckets[:, :, None] == jnp.arange(bias_table.shape[0], dtype=jnp.int32)[None, None, :]).astype(jnp.float32)
    return jnp.einsum('ijb,bh->hij', picker, bias_table, precision=highest)

def attend_block(operands, position_terms):
    query_states, key_states, value_states, segment = operands
    scores = jnp.einsum('gqhd,gkhd->ghqk', query_states, key_states, precision=highest) * score_scale + position_terms[None]
    scores = low_back(scores)
    same_doc = segment[:, :, None] == segment[:, None, :]
    scores = jnp.where(same_doc[:, None], scores, masked_score)
    weights = jax.nn.softmax(scores, axis=-1)
    return jnp.einsum('ghqk,gkhd->gqhd', low(weights), value_states, precision=highest)

def expert_apply(operands):
    expert_rows, first_weight, second_weight = operands
    inner_act = low_back(jnp.dot(expert_rows, first_weight, precision=highest))
    active = low(jax.nn.gelu(inner_act))
    return jnp.dot(active, second_weight, precision=highest)

def reference(inputs, segments, expert_index, gain_attn, query_weight, key_weight, value_weight, output_weight, bias_table, gain_ffn, router_weight, expert_in, expert_out, cotangent):
    chosen = expert_index[:, 0].astype(jnp.int32)
    picked = (chosen[:, None] == jnp.arange(EXPERTS, dtype=jnp.int32)[None, :]).astype(jnp.int32)
    per_device = picked.reshape(N_GROUP * N_LOCAL, TOK_DEV, EXPERTS)
    running = jnp.cumsum(per_device, axis=1).astype(jnp.int32)
    position = (lax.optimization_barrier(jnp.sum(running * per_device, axis=-1)) - 1).astype(jnp.int32).reshape(TOKENS)
    kept_mask = position < CAP
    source = jnp.arange(TOKENS, dtype=jnp.int32) // TOK_DEV
    slot_index = jnp.where(kept_mask, chosen * SLOTS + source * CAP + position, EXPERTS * SLOTS).astype(jnp.int32)
    expert_load = lax.optimization_barrier(jnp.sum(per_device, axis=1)).astype(jnp.int32)
    sent_rows = jnp.minimum(expert_load, CAP)
    counts = jnp.stack([lax.optimization_barrier(jnp.sum(sent_rows, axis=0)), lax.optimization_barrier(jnp.sum(expert_load - sent_rows, axis=0))]).astype(jnp.int32)
    pick_float = picked.astype(jnp.float32)
    grouped = 8
    block_count = SEQS // grouped
    head_shape = (block_count, grouped, SEQ, H, HD)

    def forward(tokens, gain_one, query_w, key_w, value_w, out_w, table_w, gain_two, router_w, first_w, second_w):
        normed = low(rms_scale(tokens, gain_one))
        query_states = low_both(jnp.dot(normed, query_w, precision=highest))
        key_states = low_both(jnp.dot(normed, key_w, precision=highest))
        value_states = low_both(jnp.dot(normed, value_w, precision=highest))
        position_terms = position_bias(table_w, SEQ)
        blocks = lax.map(jax.checkpoint(partial(attend_block, position_terms=position_terms)), (query_states.reshape(head_shape), key_states.reshape(head_shape), value_states.reshape(head_shape), segments.reshape(block_count, grouped, SEQ)))
        mixed_rows = low_both(blocks.reshape(TOKENS, D))
        attended = jnp.dot(mixed_rows, out_w, precision=highest)
        hidden = tokens + low_back(attended)
        routed = low(rms_scale(hidden, gain_two))
        logits = low_back(jnp.dot(routed, router_w, precision=highest))
        gate_values = lax.optimization_barrier(jnp.sum(jax.nn.softmax(logits, axis=-1) * pick_float, axis=-1))
        buffer = jnp.zeros((EXPERTS * SLOTS + 1, D), jnp.float32).at[slot_index].add(routed)[:-1]
        buffer = low_back(buffer).reshape(EXPERTS, SLOTS, D)
        returned = lax.map(jax.checkpoint(expert_apply), (buffer, first_w, second_w))
        returned = low_both(returned).reshape(EXPERTS * SLOTS, D)
        padded = jnp.concatenate([returned, jnp.zeros((1, D), jnp.float32)], axis=0)
        return hidden + gate_values[:, None] * padded[slot_index]
    result, pullback = jax.vjp(forward, inputs.astype(jnp.float32), gain_attn.astype(jnp.float32), query_weight.astype(jnp.float32), key_weight.astype(jnp.float32), value_weight.astype(jnp.float32), output_weight.astype(jnp.float32), bias_table.astype(jnp.float32), gain_ffn.astype(jnp.float32), router_weight.astype(jnp.float32), expert_in.astype(jnp.float32), expert_out.astype(jnp.float32))
    gradients = pullback(cotangent.astype(jnp.float32))
    return (result.astype(jnp.bfloat16), gradients[0].astype(jnp.bfloat16), gradients[1], gradients[2], gradients[3], gradients[4], gradients[5], gradients[6], gradients[7], gradients[8], gradients[9], gradients[10], counts)
```

```python
import functools

import jax
import jax.numpy as jnp
from jax import lax
from jax.experimental import pallas as pl
from jax.experimental.pallas import tpu as pltpu
from jax.sharding import PartitionSpec as P

MESH = pl.DeviceIdType.MESH
AXES = ("group", "local")
epsilon = 1e-06
score_scale = 0.125
masked_score = -1000000000.0
far_limits = (12, 16, 23, 32, 46, 64, 91)
MIB = 2**20
BF = jnp.bfloat16
F32 = jnp.float32


def nn(a, b):
    return jnp.dot(a, b, preferred_element_type=F32)


def nt(a, b):
    return lax.dot_general(a, b, (((1,), (1,)), ((), ())), preferred_element_type=F32)


def tn(a, b):
    return lax.dot_general(a, b, (((0,), (0,)), ((), ())), preferred_element_type=F32)


def iota(shape, dim):
    return lax.broadcasted_iota(jnp.int32, shape, dim)


class Plan:
    def __init__(self, n, n_local, tokens, width, experts, heads, buckets):
        self.n, self.n_local, self.tokens, self.width = n, n_local, tokens, width
        self.experts, self.heads, self.buckets = experts, heads, buckets
        self.head = width // heads
        self.cap = (5 * tokens + 4 * experts - 1) // (4 * experts)
        self.lanes = width // 128
        self.folded = 16 < self.cap <= 20 and self.lanes == 6
        self.rows = 16 if self.folded else -(-self.cap // 16) * 16
        self.packed = width + 256 if self.folded else width
        self.slots = n * self.rows
        self.extra = n * 4 if self.folded else 0

    def peer(self, me, k):
        c = (me % 2 + k % 2) % 2
        x = ((me // 2) % 2 + (k // 2) % 2) % 2
        y = ((me // 4) % 2 + (k // 4) % 2) % 2
        z = (me // 8 + k // 8) % (self.n // 8)
        return z * 8 + y * 4 + x * 2 + c

    def coords(self, d):
        return (d // self.n_local, d % self.n_local)


def me_index(plan):
    return lax.axis_index("group") * plan.n_local + lax.axis_index("local")


def greet_all(plan, me):
    barrier = pltpu.get_barrier_semaphore()

    def one(k, carry):
        pl.semaphore_signal(
            barrier, inc=1, device_id=plan.coords(plan.peer(me, k)), device_id_type=MESH
        )
        return carry

    lax.fori_loop(1, plan.n, one, 0)
    pl.semaphore_wait(barrier, plan.n - 1)


def block_copy(plan, me, k, src, dst, send_sem, recv_sem):
    target = plan.peer(me, k)
    rows = plan.rows
    return pltpu.make_async_remote_copy(
        src_ref=src.at[pl.ds(pl.multiple_of(target * rows, rows), rows), :],
        dst_ref=dst.at[pl.ds(pl.multiple_of(me * rows, rows), rows), :],
        send_sem=send_sem.at[k],
        recv_sem=recv_sem.at[k],
        device_id=plan.coords(target),
        device_id_type=MESH,
    )


def own_copy(plan, me, src, dst, sem):
    rows = plan.rows
    place = pl.ds(pl.multiple_of(me * rows, rows), rows)
    return pltpu.make_async_copy(src.at[place, :], dst.at[place, :], sem)


def start_all(plan, me, src, dst, send_sem, recv_sem):
    def one(k, carry):
        block_copy(plan, me, k, src, dst, send_sem, recv_sem).start()
        return carry

    lax.fori_loop(1, plan.n, one, 0)
    own_copy(plan, me, src, dst, send_sem.at[0]).start()


def wait_all(plan, me, src, dst, send_sem, recv_sem):
    def one(k, carry):
        block_copy(plan, me, k, src, dst, send_sem, recv_sem).wait()
        return carry

    lax.fori_loop(1, plan.n, one, 0)
    own_copy(plan, me, src, dst, send_sem.at[0]).wait()


def slot_rows(plan, ids):
    slot = iota((plan.slots, plan.tokens), 0).astype(F32)
    main = jnp.where(slot == ids[1:2, :], 1.0, 0.0).astype(BF)
    if not plan.folded:
        return main, None
    place = iota((plan.slots, plan.tokens), 0)
    folded = ((place // 16) * 4 + place % 4).astype(F32)
    return main, jnp.where(folded == ids[2:3, :], 1.0, 0.0).astype(BF)


def fold(plan, full, count):
    part = (iota((count, 128), 0) % 16) // 4
    first = jnp.where(part == 0, full[:, 0:128], 0.0)
    for g in range(1, 4):
        first = jnp.where(part == g, full[:, 128 * g : 128 * g + 128], first)
    second = jnp.where(part == 0, full[:, 512:640], jnp.where(part == 1, full[:, 640:768], 0.0))
    return first, second


def dispatch_to(plan, dmain, dextra, values, out_ref):
    out_ref[:, 0 : plan.width] = nn(dmain, values).astype(BF)
    if plan.folded:
        first, second = fold(plan, nn(dextra, values), plan.slots)
        out_ref[:, 768:896] = first.astype(BF)
        out_ref[:, 896:1024] = second.astype(BF)


def token_slots(plan, eidx_row):
    t, e = plan.tokens, plan.experts
    pick = jnp.where(eidx_row == iota((e, t), 0), 1.0, 0.0)
    upper = jnp.where(iota((t, t), 0) <= iota((t, t), 1), 1.0, 0.0).astype(BF)
    running = nn(pick.astype(BF), upper)
    position = jnp.sum(running * pick, axis=0, keepdims=True) - 1.0
    chosen = eidx_row.astype(F32)
    if plan.folded:
        main = jnp.where(position < 16.0, chosen * 16.0 + position, -1.0)
        extra = jnp.where(
            (position >= 16.0) & (position < plan.cap), chosen * 4.0 + (position - 16.0), -1.0
        )
    else:
        main = jnp.where(position < plan.cap, chosen * float(plan.rows) + position, -1.0)
        extra = jnp.full_like(main, -1.0)
    row = iota((128, t), 0)
    return jnp.where(
        row == 1, main, jnp.where(row == 2, extra, jnp.where(row == 3, chosen, 0.0))
    )


def bucket_rows(shape, offset):
    distance = jnp.abs(offset)
    far = jnp.zeros(shape, jnp.int32) + 8
    for threshold in far_limits:
        far = far + (distance >= threshold).astype(jnp.int32)
    return jnp.where(distance < 8, distance, far) + 16 * (offset > 0).astype(jnp.int32)


def bucket_onehot(buckets, span):
    lane = iota((buckets, span), 1)
    signed = jnp.where(lane < 896, 384 - lane, 384 + span - lane)
    return jnp.where(bucket_rows((buckets, span), signed) == iota((buckets, span), 0), 1.0, 0.0)


def rms(values):
    return lax.rsqrt(jnp.mean(values * values, axis=-1, keepdims=True) + epsilon)


SPAN = 1024


def forward_kernel(
    plan,
    x_ref, seg_ref, eidx_ref, g1_ref, wq_ref, wk_ref, wv_ref, wo_ref, table_ref, g2_ref, rw_ref, ct_ref,
    ct_recv, routed_out, e_out, rinv_out, normed_out, q_out, k_out, v_out, mixed_out, hidden_out, aux_out,
    ct_send, skew, mask, s_buf, e_buf, vt, mixt, send_sem, recv_sem, e_sem,
):
    t = plan.tokens
    me = me_index(plan)
    greet_all(plan, me)

    ids = token_slots(plan, eidx_ref[...])
    dmain, dextra = slot_rows(plan, ids)
    dispatch_to(plan, dmain, dextra, ct_ref[...], ct_send)
    start_all(plan, me, ct_send, ct_recv, send_sem, recv_sem)

    tokens = x_ref[...].astype(F32)
    normed = (tokens * rms(tokens) * g1_ref[...]).astype(BF)
    normed_out[...] = normed
    q_out[...] = (nn(normed, wq_ref[...]).astype(BF).astype(F32) * score_scale).astype(BF)
    k_out[...] = nn(normed, wk_ref[...]).astype(BF)
    v_out[...] = nn(normed, wv_ref[...]).astype(BF)
    vt[...] = v_out[...].T

    base = jnp.dot(
        table_ref[...],
        bucket_onehot(plan.buckets, SPAN),
        precision=lax.Precision.HIGHEST,
        preferred_element_type=F32,
    )
    for h in range(plan.heads):
        row = jnp.broadcast_to(base[h : h + 1, :], (128, SPAN))
        skew[h] = pltpu.roll(row, 0, 1, stride=1, stride_axis=0)
    seg_row = seg_ref[...].astype(F32)
    seg_col = jnp.broadcast_to(seg_row, (128, t)).T[:, 0:1]
    mask[...] = jnp.where(seg_col == seg_row, 0.0, masked_score)

    def pair(p, carry):
        lanes = pl.ds(pl.multiple_of(p * 128, 128), 128)
        for side in range(2):
            h = 2 * p + side
            keep = (iota((t, 128), 1) // 64) == side
            qm = jnp.where(keep, q_out[:, lanes], jnp.zeros((), BF))
            for ib in range(t // 256):
                cols = slice(256 * ib, 256 * ib + 256)
                top = jnp.full((8, 256), -3.0e38, F32)
                for jb in range(t // 128):
                    rows = slice(128 * jb, 128 * jb + 128)
                    start = 384 - 128 * jb + 256 * ib
                    s = nt(k_out[rows, lanes], qm[cols, :])
                    s = s + skew[h, :, start : start + 256] + mask[rows, cols]
                    s_buf[rows, cols] = s
                    top = jnp.maximum(top, jnp.max(s.reshape(16, 8, 256), axis=0))
                top = jnp.max(top, axis=0, keepdims=True)
                total = jnp.zeros((8, 256), F32)
                for jb in range(t // 128):
                    rows = slice(128 * jb, 128 * jb + 128)
                    ex = jnp.exp(s_buf[rows, cols] - top)
                    e_buf[h, rows, cols] = ex.astype(BF)
                    total = total + jnp.sum(ex.reshape(16, 8, 256), axis=0)
                rinv_out[pl.ds(h, 1), cols] = 1.0 / jnp.sum(total, axis=0, keepdims=True)
            pltpu.make_async_copy(e_buf.at[h], e_out.at[h], e_sem.at[h]).start()
            place = pl.ds(pl.multiple_of(p * 128 + side * 64, 64), 64)
            mixed = nn(vt[place, :], e_buf[h]) * rinv_out[pl.ds(h, 1), :]
            mixt[place, :] = mixed.astype(BF)
        return carry

    lax.fori_loop(0, plan.heads // 2, pair, 0)
    mixed_out[...] = mixt[...].T
    hidden = tokens + nn(mixed_out[...], wo_ref[...])
    hidden_out[...] = hidden
    routed = (hidden * rms(hidden) * g2_ref[...]).astype(BF)
    logits = nt(routed, rw_ref[...])
    grown = jnp.exp(logits - jnp.max(logits, axis=1, keepdims=True))
    probs = grown / jnp.sum(grown, axis=1, keepdims=True)
    columns = ids.T
    pick = columns[:, 3:4] == iota((t, plan.experts), 1).astype(F32)
    gate = jnp.sum(jnp.where(pick, probs, 0.0), axis=1, keepdims=True)
    aux_out[...] = jnp.where(iota((t, 128), 1) == 0, gate, columns)
    dispatch_to(plan, dmain, dextra, routed, routed_out)

    def drain(h, carry):
        pltpu.make_async_copy(e_buf.at[h], e_out.at[h], e_sem.at[h]).wait()
        return carry

    lax.fori_loop(0, plan.heads, drain, 0)
    wait_all(plan, me, ct_send, ct_recv, send_sem, recv_sem)


def forward_part(plan, x, seg, eidx, g1, wq, wk, wv, wo, table, g2, rw, ct):
    t, w, h = plan.tokens, plan.width, plan.heads
    block = jax.ShapeDtypeStruct((plan.slots, plan.packed), BF)
    state = jax.ShapeDtypeStruct((t, w), BF)
    vmem = pl.BlockSpec(memory_space=pltpu.VMEM)
    any_ = pl.BlockSpec(memory_space=pl.ANY)
    return pl.pallas_call(
        functools.partial(forward_kernel, plan),
        out_shape=(
            block, block,
            jax.ShapeDtypeStruct((h, t, t), BF),
            jax.ShapeDtypeStruct((16, t), F32),
            state, state, state, state, state,
            jax.ShapeDtypeStruct((t, w), F32),
            jax.ShapeDtypeStruct((t, 128), F32),
        ),
        in_specs=[vmem] * 12,
        out_specs=(any_, vmem, any_) + (vmem,) * 8,
        scratch_shapes=[
            pltpu.VMEM((plan.slots, plan.packed), BF),
            pltpu.VMEM((h, 128, SPAN), F32),
            pltpu.VMEM((t, t), F32),
            pltpu.VMEM((t, t), F32),
            pltpu.VMEM((h, t, t), BF),
            pltpu.VMEM((w, t), BF),
            pltpu.VMEM((w, t), BF),
            pltpu.SemaphoreType.DMA((plan.n,)),
            pltpu.SemaphoreType.DMA((plan.n,)),
            pltpu.SemaphoreType.DMA((h,)),
        ],
        compiler_params=pltpu.CompilerParams(
            collective_id=0, has_side_effects=True, vmem_limit_bytes=60 * MIB
        ),
        name="forward_attention",
    )(x, seg, eidx, g1, wq, wk, wv, wo, table, g2, rw, ct)


def unfold_picks(count, g):
    row = iota((count // 4, count), 0)
    place = (row // 4) * 16 + g * 4 + row % 4
    return jnp.where(iota((count // 4, count), 1) == place, 1.0, 0.0).astype(BF)


def unfold(lanes, count):
    parts = [nn(unfold_picks(count, g), lanes) for g in range(4)]
    return jnp.concatenate(
        [parts[0][:, 0:128], parts[1][:, 0:128], parts[2][:, 0:128], parts[3][:, 0:128],
         parts[0][:, 128:256], parts[1][:, 128:256]],
        axis=1,
    ).astype(BF)


def refold(plan, rows, count):
    row = iota((count, count // 4), 0)
    place = (row // 16) * 4 + row % 4
    picks = jnp.where(iota((count, count // 4), 1) == place, 1.0, 0.0).astype(BF)
    return fold(plan, nn(picks, rows), count)


def expert_kernel(
    plan, span,
    routed_ref, ct_ref, w1_hbm, w2_hbm, rw_ref,
    home_out, ret_out, rows_out, gret_out, act_out, gi_out, rgrad_out,
    land, ct, w1, w2, act, gi, ret_acc, grow, gsend, gl_all,
    send_sem, recv_sem, back_send, back_recv, w_sem, ct_sem, out_sem,
):
    me = me_index(plan)
    planes = plan.n // 8
    main_rows = 8 * plan.rows
    plane_rows = main_rows + (32 if plan.folded else 0)
    group = span * plane_rows
    z = me // 8
    ff = w1_hbm.shape[2]
    step = 512

    load1 = pltpu.make_async_copy(w1_hbm.at[0], w1, w_sem.at[0])
    load2 = pltpu.make_async_copy(w2_hbm.at[0], w2, w_sem.at[1])
    load3 = pltpu.make_async_copy(ct_ref, ct, ct_sem)
    load3.start()
    load1.start()
    load2.start()
    greet_all(plan, me)
    start_all(plan, me, routed_ref, land, send_sem, recv_sem)
    load3.wait()

    def place_of(kz):
        source = (z + planes - kz) % planes
        return pl.ds(pl.multiple_of(source * main_rows, main_rows), main_rows)

    def assemble(kz, packed, target):
        base = kz * plane_rows
        place = place_of(kz)
        target[base : base + main_rows, :] = packed[place, 0 : plan.width]
        if plan.folded:
            target[base + main_rows : base + plane_rows, :] = unfold(
                packed[place, 768:1024], main_rows
            )

    def pack(kz, values, target):
        place = place_of(kz)
        target[place, 0 : plan.width] = values[0:main_rows, :]
        if plan.folded:
            first, second = refold(plan, values[main_rows:plane_rows, :], main_rows)
            target[place, 768:896] = first.astype(BF)
            target[place, 896:1024] = second.astype(BF)

    for first in range(0, planes, span):
        for kz in range(first, first + span):
            if kz == 0:
                own_copy(plan, me, routed_ref, land, send_sem.at[0]).wait()
            def arrived(low, carry, kz=kz):
                block_copy(plan, me, kz * 8 + low, routed_ref, land, send_sem, recv_sem).wait_recv()
                return carry
            lax.fori_loop(1 if kz == 0 else 0, 8, arrived, 0)
            assemble(kz, land, rows_out)
            assemble(kz, ct, gret_out)
        if first == 0:
            load1.wait()
            load2.wait()
        mine = slice(first * plane_rows, first * plane_rows + group)
        rows = rows_out[mine, :]
        raw = gret_out[mine, :]
        logits = nt(rows, rw_ref[...])
        grown = jnp.exp(logits - jnp.max(logits, axis=1, keepdims=True))
        probs = grown / jnp.sum(grown, axis=1, keepdims=True)
        chosen = jnp.where(iota((group, plan.experts), 1) == me, 1.0, 0.0)
        gate = jnp.sum(probs * chosen, axis=1, keepdims=True)
        gret_out[mine, :] = (gate * raw.astype(F32)).astype(BF)
        for at in range(0, ff, step):
            cols = slice(at, at + step)
            inner = nn(rows_out[mine, :], w1[:, cols])
            grad = nt(gret_out[mine, :], w2[cols, :])
            square = inner * inner
            slope = 0.7978845608028654 + 0.1070322244 * square
            tanh = jnp.tanh(inner * (0.7978845608028654 + 0.035677408136300125 * square))
            half = 0.5 + 0.5 * tanh
            act[mine, cols] = (inner * half).astype(BF)
            gi[mine, cols] = (grad * (half + 0.5 * inner * (1.0 - tanh * tanh) * slope)).astype(BF)
            if at == 0:
                ret_acc[...] = nn(act[mine, cols], w2[cols, :])
                grow[...] = nt(gi[mine, cols], w1[:, cols])
            else:
                ret_acc[...] += nn(act[mine, cols], w2[cols, :])
                grow[...] += nt(gi[mine, cols], w1[:, cols])
        answer = ret_acc[...].astype(BF)
        grad_gate = jnp.sum(raw.astype(F32) * answer.astype(F32), axis=1, keepdims=True)
        grad_logits = (probs * (chosen - gate) * grad_gate).astype(BF)
        gl_all[mine, :] = grad_logits
        back = (grow[...] + nn(grad_logits, rw_ref[...])).astype(BF)
        for kz in range(first, first + span):
            part = slice((kz - first) * plane_rows, (kz - first + 1) * plane_rows)
            pack(kz, back[part, :], gsend)
            if kz == 0:
                own_copy(plan, me, gsend, home_out, back_send.at[0]).start()
            def send(low, carry, kz=kz):
                k = ((planes - kz) % planes) * 8 + low
                block_copy(plan, me, k, gsend, home_out, back_send, back_recv).start()
                return carry
            lax.fori_loop(1 if kz == 0 else 0, 8, send, 0)
            pack(kz, answer[part, :], ret_out)
        pltpu.make_async_copy(
            act.at[mine, :], act_out.at[mine, :], out_sem.at[2 * (first // span)]
        ).start()
        pltpu.make_async_copy(
            gi.at[mine, :], gi_out.at[mine, :], out_sem.at[2 * (first // span) + 1]
        ).start()
    rgrad_out[...] = tn(gl_all[...], rows_out[...])
    for first in range(0, planes, span):
        mine = slice(first * plane_rows, first * plane_rows + group)
        pltpu.make_async_copy(
            act.at[mine, :], act_out.at[mine, :], out_sem.at[2 * (first // span)]
        ).wait()
        pltpu.make_async_copy(
            gi.at[mine, :], gi_out.at[mine, :], out_sem.at[2 * (first // span) + 1]
        ).wait()

    def sent(k, carry):
        block_copy(plan, me, k, routed_ref, land, send_sem, recv_sem).wait_send()
        return carry

    lax.fori_loop(1, plan.n, sent, 0)
    wait_all(plan, me, gsend, home_out, back_send, back_recv)


def expert_part(plan, routed, ct, w1, w2, rw):
    span = 2 if plan.n == 32 else 1
    planes = plan.n // 8
    total = plan.slots + plan.extra
    group = span * total // planes
    ff, w, e = w1.shape[2], plan.width, plan.experts
    vmem = pl.BlockSpec(memory_space=pltpu.VMEM)
    any_ = pl.BlockSpec(memory_space=pl.ANY)
    block = jax.ShapeDtypeStruct((plan.slots, plan.packed), BF)
    return pl.pallas_call(
        functools.partial(expert_kernel, plan, span),
        out_shape=(
            block, block,
            jax.ShapeDtypeStruct((total, w), BF),
            jax.ShapeDtypeStruct((total, w), BF),
            jax.ShapeDtypeStruct((total, ff), BF),
            jax.ShapeDtypeStruct((total, ff), BF),
            jax.ShapeDtypeStruct((e, w), F32),
        ),
        in_specs=[any_] * 4 + [vmem],
        out_specs=(any_, vmem, vmem, vmem, any_, any_, vmem),
        scratch_shapes=[
            pltpu.VMEM((plan.slots, plan.packed), BF),
            pltpu.VMEM((plan.slots, plan.packed), BF),
            pltpu.VMEM((w, ff), BF),
            pltpu.VMEM((ff, w), BF),
            pltpu.VMEM((total, ff), BF),
            pltpu.VMEM((total, ff), BF),
            pltpu.VMEM((group, w), F32),
            pltpu.VMEM((group, w), F32),
            pltpu.VMEM((plan.slots, plan.packed), BF),
            pltpu.VMEM((total, e), BF),
            pltpu.SemaphoreType.DMA((plan.n,)),
            pltpu.SemaphoreType.DMA((plan.n,)),
            pltpu.SemaphoreType.DMA((plan.n,)),
            pltpu.SemaphoreType.DMA((plan.n,)),
            pltpu.SemaphoreType.DMA((2,)),
            pltpu.SemaphoreType.DMA,
            pltpu.SemaphoreType.DMA((2 * planes,)),
        ],
        compiler_params=pltpu.CompilerParams(
            collective_id=1, has_side_effects=True, vmem_limit_bytes=60 * MIB
        ),
        name="expert_exchange",
    )(routed, ct, w1, w2, rw)


def weight_grad_kernel(rows_ref, gret_ref, act_ref, gi_ref, in_ref, out_ref):
    in_ref[0] = tn(rows_ref[...], gi_ref[...])
    out_ref[0] = tn(act_ref[...], gret_ref[...])


def weight_grads(plan, rows, gret, act, gi):
    total, w = rows.shape
    ff = act.shape[1]
    step = 512
    return pl.pallas_call(
        weight_grad_kernel,
        out_shape=(
            jax.ShapeDtypeStruct((1, w, ff), F32),
            jax.ShapeDtypeStruct((1, ff, w), F32),
        ),
        grid=(ff // step,),
        in_specs=[
            pl.BlockSpec((total, w), lambda i: (0, 0)),
            pl.BlockSpec((total, w), lambda i: (0, 0)),
            pl.BlockSpec((total, step), lambda i: (0, i)),
            pl.BlockSpec((total, step), lambda i: (0, i)),
        ],
        out_specs=(
            pl.BlockSpec((1, w, step), lambda i: (0, 0, i)),
            pl.BlockSpec((1, step, w), lambda i: (0, i, 0)),
        ),
        compiler_params=pltpu.CompilerParams(vmem_limit_bytes=40 * MIB),
        name="expert_weight_grads",
    )(rows, gret, act, gi)


class Reducer:
    def __init__(self, plan, me, src, near, near_vmem, mid, far, out, sems, slot, dtype):
        self.plan, self.me, self.src, self.out, self.dtype = plan, me, src, out, dtype
        self.near, self.near_vmem, self.mid, self.far = near, near_vmem, mid, far
        self.sems, self.slot = sems, slot
        rows = src.shape[0]
        self.half, self.quarter, self.own = rows // 2, rows // 8, rows // plan.n
        self.depth = plan.n // 8
        self.core, self.chip, self.z = me % 2, (me // 2) % 4, me // 8
        self.half_at = self.core * self.half
        self.quarter_at = self.half_at + self.chip * self.quarter
        self.own_at = self.quarter_at + self.z * self.own

    def span(self, start, size):
        return pl.ds(pl.multiple_of(start, self.own), size)

    def remote(self, src, dst, level, index, peer):
        send, recv = self.sems
        place = level + index
        return pltpu.make_async_remote_copy(
            src_ref=src, dst_ref=dst,
            send_sem=send.at[self.slot, place], recv_sem=recv.at[self.slot, place],
            device_id=self.plan.coords(peer), device_id_type=MESH,
        )

    def cross(self):
        peer = self.plan.peer(self.me, 1)
        return [self.remote(
            self.src.at[self.span((1 - self.core) * self.half, self.half), :], self.near, 0, 0, peer
        )]

    def plane(self):
        copies = []
        for o in range(1, 4):
            peer = self.plan.peer(self.me, 2 * o)
            at = self.half_at + ((peer // 2) % 4) * self.quarter
            copies.append(self.remote(
                self.src.at[self.span(at, self.quarter), :], self.mid.at[o - 1], 1, o - 1, peer
            ))
        return copies

    def along(self):
        copies = []
        for o in range(1, self.depth):
            peer = self.plan.peer(self.me, 8 * o)
            at = self.quarter_at + (peer // 8) * self.own
            copies.append(self.remote(
                self.src.at[self.span(at, self.own), :], self.far.at[o - 1], 8, o - 1, peer
            ))
        return copies

    def along_back(self):
        place = self.span(self.own_at, self.own)
        return [
            self.remote(self.src.at[place, :], self.out.at[place, :], 8 + self.depth, o - 1,
                        self.plan.peer(self.me, 8 * o))
            for o in range(1, self.depth)
        ]

    def own_local(self):
        place = self.span(self.own_at, self.own)
        return pltpu.make_async_copy(
            self.src.at[place, :], self.out.at[place, :], self.sems[0].at[self.slot, 7]
        )

    def plane_back(self):
        place = self.span(self.quarter_at, self.quarter)
        return [
            self.remote(self.out.at[place, :], self.out.at[place, :], 4, o - 1,
                        self.plan.peer(self.me, 2 * o))
            for o in range(1, 4)
        ]

    def cross_back(self):
        place = self.span(self.half_at, self.half)
        return [self.remote(
            self.out.at[place, :], self.out.at[place, :], 8 + 2 * self.depth, 0,
            self.plan.peer(self.me, 1),
        )]

    def add(self, start, size, parts):
        place = self.span(start, size)
        total = self.src[place, :].astype(F32)
        for part in parts:
            total = total + part.astype(F32)
        self.src[place, :] = total.astype(self.dtype)

    def step(self, number):
        if number == 0:
            for c in self.cross():
                c.start()
        elif number == 1:
            for c in self.cross():
                c.wait()
            if self.near_vmem is None:
                near = self.near
            else:
                near = self.near_vmem
                fetch = pltpu.make_async_copy(self.near, near, self.sems[1].at[self.slot, 7])
                fetch.start()
                fetch.wait()
            self.add(self.half_at, self.half, [near[...]])
            for c in self.plane():
                c.start()
        elif number == 2:
            for c in self.plane():
                c.wait()
            self.add(self.quarter_at, self.quarter, [self.mid[o] for o in range(3)])
            for c in self.along():
                c.start()
        elif number == 3:
            for c in self.along():
                c.wait()
            self.add(self.own_at, self.own, [self.far[o] for o in range(self.depth - 1)])
            self.own_local().start()
            for c in self.along_back():
                c.start()
        elif number == 4:
            self.own_local().wait()
            for c in self.along_back():
                c.wait()
            for c in self.plane_back():
                c.start()
        elif number == 5:
            for c in self.plane_back():
                c.wait()
            for c in self.cross_back():
                c.start()
        else:
            for c in self.cross_back():
                c.wait()


def small_places(plan):
    e = plan.experts
    ffn = plan.lanes * e
    attn, table, counts = ffn + 8, ffn + 16, ffn + 32
    unit = 8 * plan.n
    return ffn, attn, table, counts, -(-(counts + 8) // unit) * unit


def diagonal_sums(block):
    size = 64
    while size >= 8:
        block = block[0:size, :] + pltpu.roll(block[size : 2 * size, :], SPAN - size, 1)
        size //= 2
    row = iota((8, SPAN), 0)
    for bit in (4, 2, 1):
        block = jnp.where((row // bit) % 2 == 1, pltpu.roll(block, SPAN - bit, 1), block)
    return jnp.sum(block, axis=0, keepdims=True)


def norm_back(values, scale, gain, grad):
    weighted = gain * grad
    inner = jnp.mean(weighted * values, axis=-1, keepdims=True)
    back = scale * weighted - values * (scale * scale * scale * inner)
    return back, jnp.sum(grad * values * scale, axis=0, keepdims=True)


def backward_kernel(
    plan, schedule,
    home_ref, ret_ref, e_hbm, rinv_ref, normed_ref, q_ref, k_ref, v_ref, mixed_ref, hidden_ref, aux_ref, eidx_ref,
    x_ref, ct_ref, wq_ref, wk_ref, wv_ref, wo_ref, g1_ref, g2_ref, rgrad_ref,
    output_out, input_out, flat_out, small_out, near_hbm,
    home, ret, e_buf, dp_buf, ds_buf, skew, diag, scaled, across, dqt, dq, dk, dv, grad_hidden,
    flat, near, mid, far, small, s_near, s_mid, s_far,
    send_sem, recv_sem, e_sem, home_sem, ar_send, ar_recv,
):
    t, w = plan.tokens, plan.width
    me = me_index(plan)
    load_home = pltpu.make_async_copy(home_ref, home, home_sem)
    load_home.start()

    def load_e(h):
        return pltpu.make_async_copy(e_hbm.at[h], e_buf.at[h], e_sem.at[h])

    for h in range(plan.heads):
        load_e(h).start()
    greet_all(plan, me)
    start_all(plan, me, ret_ref, ret, send_sem, recv_sem)

    sums = [
        Reducer(plan, me, flat.at[c], near_hbm.at[c], near, mid.at[c], far.at[c], flat_out.at[c],
                (ar_send, ar_recv), c, BF)
        for c in range(4)
    ]
    sums.append(Reducer(plan, me, small, s_near, None, s_mid, s_far, small_out, (ar_send, ar_recv), 4, F32))

    def advance(moment):
        for c, number in schedule.get(moment, ()):
            sums[c].step(number)

    rows_full = plan.lanes * w
    if flat.shape[1] > rows_full:
        for c in range(4):
            flat[c, rows_full:, :] = jnp.zeros((flat.shape[1] - rows_full, 128), BF)

    aux = aux_ref[...]
    gate = aux[:, 0:1]
    dmain = jnp.where(iota((t, plan.slots), 1).astype(F32) == aux[:, 1:2], 1.0, 0.0).astype(BF)
    if plan.folded:
        dextra = jnp.where(iota((t, plan.extra), 1).astype(F32) == aux[:, 2:3], 1.0, 0.0).astype(BF)

    def combine(packed):
        total = nn(dmain, packed[:, 0:w])
        if plan.folded:
            total = total + nn(dextra, unfold(packed[:, 768:1024], plan.slots))
        return total

    hidden = hidden_ref[...]
    across[...] = mixed_ref[...].T
    load_home.wait()
    back, gain_ffn = norm_back(hidden, rms(hidden), g2_ref[...], combine(home))
    grad_hidden[...] = ct_ref[...].astype(F32) + back
    attended = grad_hidden[...].astype(BF)
    for b in range(w // 256):
        part = nn(across[...], attended[:, 256 * b : 256 * b + 256]).astype(BF)
        flat[0, 2 * b * w : (2 * b + 1) * w, :] = part[:, 0:128]
        flat[0, (2 * b + 1) * w : (2 * b + 2) * w, :] = part[:, 128:256]
    advance("out")
    spread = jnp.where(iota((16, w), 1) // plan.head == iota((16, w), 0), 1.0, 0.0)
    shares = jnp.dot(
        rinv_ref[...].T, spread, precision=lax.Precision.HIGHEST, preferred_element_type=F32
    )
    scaled[...] = (nt(attended, wo_ref[...]).astype(BF).astype(F32) * shares).astype(BF)
    dqt[...] = k_ref[...].T
    across[...] = normed_ref[...].T
    skew[:, t + 384 :] = jnp.zeros((128, SPAN - t - 384), F32)

    for p in range(plan.heads // 2):
        lanes = slice(128 * p, 128 * p + 128)
        dk_pair = jnp.zeros((t, 128), F32)
        dv_pair = jnp.zeros((t, 128), F32)
        for side in range(2):
            h = 2 * p + side
            keep = (iota((t, 128), 1) // 64) == side
            dom = jnp.where(keep, scaled[:, lanes], jnp.zeros((), BF))
            qm = jnp.where(keep, q_ref[:, lanes], jnp.zeros((), BF))
            load_e(h).wait()
            skew[:, 0 : t + 384] = jnp.zeros((128, t + 384), F32)
            for ib in range(t // 256):
                cols = slice(256 * ib, 256 * ib + 256)
                delta = jnp.zeros((8, 256), F32)
                for jb in range(t // 128):
                    rows = slice(128 * jb, 128 * jb + 128)
                    dp = nt(v_ref[rows, lanes], dom[cols, :])
                    dp_buf[rows, cols] = dp
                    prod = dp * e_buf[h, rows, cols].astype(F32)
                    delta = delta + jnp.sum(prod.reshape(16, 8, 256), axis=0)
                delta = jnp.sum(delta, axis=0, keepdims=True) * rinv_ref[h : h + 1, cols]
                for jb in range(t // 128):
                    rows = slice(128 * jb, 128 * jb + 128)
                    start = 384 - 128 * jb + 256 * ib
                    ds = e_buf[h, rows, cols].astype(F32) * (dp_buf[rows, cols] - delta)
                    ds_buf[rows, cols] = ds.astype(BF)
                    skew[:, start : start + 256] += ds
            dv_pair = dv_pair + nn(e_buf[h], dom)
            dk_pair = dk_pair + nn(ds_buf[...], qm)
            place = slice(64 * h, 64 * h + 64)
            dqt[place, :] = (nn(dqt[place, :], ds_buf[...]) * score_scale).astype(BF)
            diag[h : h + 1, :] = diagonal_sums(skew[...])
        dv[:, lanes] = dv_pair.astype(BF)
        dk[:, lanes] = dk_pair.astype(BF)
        dq[:, lanes] = dqt[128 * p : 128 * p + 128, :].T
        if p % 2 == 1:
            c = 1 + p // 2
            cols = slice(256 * (p // 2), 256 * (p // 2) + 256)
            for m, rows in enumerate((dq, dk, dv)):
                part = nn(across[...], rows[:, cols]).astype(BF)
                flat[c, 2 * m * w : (2 * m + 1) * w, :] = part[:, 0:128]
                flat[c, (2 * m + 1) * w : (2 * m + 2) * w, :] = part[:, 128:256]
        advance(p)

    grad_normed = nt(dq[...], wq_ref[...]) + nt(dk[...], wk_ref[...]) + nt(dv[...], wv_ref[...])
    tokens = x_ref[...].astype(F32)
    back, gain_attn = norm_back(tokens, rms(tokens), g1_ref[...], grad_normed)
    input_out[...] = (grad_hidden[...] + back).astype(BF)

    ffn, attn, table, counts, total = small_places(plan)
    small[ffn:, :] = jnp.zeros((total - ffn, 128), F32)
    e = plan.experts
    for g in range(plan.lanes):
        lanes = slice(128 * g, 128 * g + 128)
        small[e * g : e * g + e, :] = rgrad_ref[:, lanes]
        small[ffn + g : ffn + g + 1, :] = gain_ffn[:, lanes]
        small[attn + g : attn + g + 1, :] = gain_attn[:, lanes]
    buckets = bucket_onehot(plan.buckets, SPAN)
    sums_table = lax.dot_general(
        diag[0:plan.heads, :], buckets, (((1,), (1,)), ((), ())),
        precision=lax.Precision.HIGHEST, preferred_element_type=F32,
    )
    small[table : table + plan.heads, 0 : plan.buckets] = sums_table
    pick = jnp.where(eidx_ref[...] == iota((e, t), 0), 1.0, 0.0).astype(BF)
    load = nt(jnp.ones((8, t), BF), pick)[0:1, :]
    kept = jnp.minimum(load, float(plan.cap))
    small[counts : counts + 1, 0:e] = kept
    small[counts + 1 : counts + 2, 0:e] = load - kept
    advance("small")

    wait_all(plan, me, ret_ref, ret, send_sem, recv_sem)
    output_out[...] = (hidden_ref[...] + gate * combine(ret)).astype(BF)
    advance("tail")


SCHEDULE = {
    "out": ((0, 0),),
    0: ((0, 1),),
    1: ((1, 0), (0, 2)),
    2: ((1, 1), (0, 3)),
    3: ((2, 0), (1, 2), (0, 4)),
    4: ((2, 1), (1, 3), (0, 5)),
    5: ((3, 0), (2, 2), (1, 4)),
    "small": ((4, 0), (3, 1), (2, 3), (1, 5)),
    "tail": (
        (4, 1), (3, 2), (4, 2), (2, 4), (3, 3), (4, 3), (2, 5), (3, 4), (4, 4), (3, 5), (4, 5),
        (0, 6), (1, 6), (2, 6), (3, 6), (4, 6),
    ),
}


def backward_part(plan, home, ret, e, rinv, normed, q, k, v, mixed, hidden, aux, eidx, x, ct, wq, wk, wv, wo, g1, g2, rgrad):
    t, w, h, n = plan.tokens, plan.width, plan.heads, plan.n
    unit = 16 * n
    rows = -(-plan.lanes * w // unit) * unit
    small = small_places(plan)[-1]
    depth = n // 8
    places = 9 + 2 * depth
    vmem = pl.BlockSpec(memory_space=pltpu.VMEM)
    any_ = pl.BlockSpec(memory_space=pl.ANY)
    state = jax.ShapeDtypeStruct((t, w), BF)
    return pl.pallas_call(
        functools.partial(backward_kernel, plan, SCHEDULE),
        out_shape=(
            state, state,
            jax.ShapeDtypeStruct((4, rows, 128), BF),
            jax.ShapeDtypeStruct((small, 128), F32),
            jax.ShapeDtypeStruct((4, rows // 2, 128), BF),
        ),
        in_specs=[any_] * 3 + [vmem] * 18,
        out_specs=(vmem, vmem, any_, any_, any_),
        scratch_shapes=[
            pltpu.VMEM((plan.slots, plan.packed), BF),
            pltpu.VMEM((plan.slots, plan.packed), BF),
            pltpu.VMEM((h, t, t), BF),
            pltpu.VMEM((t, t), F32),
            pltpu.VMEM((t, t), BF),
            pltpu.VMEM((128, SPAN), F32),
            pltpu.VMEM((16, SPAN), F32),
            pltpu.VMEM((t, w), BF),
            pltpu.VMEM((w, t), BF),
            pltpu.VMEM((w, t), BF),
            pltpu.VMEM((t, w), BF),
            pltpu.VMEM((t, w), BF),
            pltpu.VMEM((t, w), BF),
            pltpu.VMEM((t, w), F32),
            pltpu.VMEM((4, rows, 128), BF),
            pltpu.VMEM((rows // 2, 128), BF),
            pltpu.VMEM((4, 3, rows // 8, 128), BF),
            pltpu.VMEM((4, max(depth - 1, 1), rows // n, 128), BF),
            pltpu.VMEM((small, 128), F32),
            pltpu.VMEM((small // 2, 128), F32),
            pltpu.VMEM((3, small // 8, 128), F32),
            pltpu.VMEM((max(depth - 1, 1), small // n, 128), F32),
            pltpu.SemaphoreType.DMA((n,)),
            pltpu.SemaphoreType.DMA((n,)),
            pltpu.SemaphoreType.DMA((h,)),
            pltpu.SemaphoreType.DMA,
            pltpu.SemaphoreType.DMA((5, places)),
            pltpu.SemaphoreType.DMA((5, places)),
        ],
        compiler_params=pltpu.CompilerParams(
            collective_id=2, has_side_effects=True, vmem_limit_bytes=60 * MIB
        ),
        name="backward_attention",
    )(home, ret, e, rinv, normed, q, k, v, mixed, hidden, aux, eidx, x, ct, wq, wk, wv, wo, g1, g2, rgrad)


def finish_kernel(plan, f0, f1, f2, f3, small_ref, out_ref, q_ref, k_ref, v_ref, g1_ref, g2_ref, table_ref, rw_ref, counts_ref):
    out_ref[...] = f0[0].astype(F32)
    q_ref[...] = f1[0].astype(F32)
    k_ref[...] = f2[0].astype(F32)
    v_ref[...] = f3[0].astype(F32)
    ffn, attn, table, counts, _ = small_places(plan)
    e = plan.experts

    @pl.when(pl.program_id(0) == 0)
    def _():
        for g in range(plan.lanes):
            lanes = slice(128 * g, 128 * g + 128)
            rw_ref[:, lanes] = small_ref[e * g : e * g + e, :]
            g2_ref[:, lanes] = small_ref[ffn + g : ffn + g + 1, :]
            g1_ref[:, lanes] = small_ref[attn + g : attn + g + 1, :]
        table_ref[...] = small_ref[table : table + plan.heads, 0 : plan.buckets]
        counts_ref[...] = small_ref[counts : counts + 2, 0:e].astype(jnp.int32)


def finish_part(plan, flat, small):
    w = plan.width
    square = jax.ShapeDtypeStruct((w, w), F32)

    def spec(m):
        return pl.BlockSpec((1, w, 128), lambda i: (1 + i // 2, 2 * m + i % 2, 0))

    whole = lambda shape: pl.BlockSpec(shape, lambda i: (0, 0))
    column = pl.BlockSpec((w, 128), lambda i: (0, i))
    return pl.pallas_call(
        functools.partial(finish_kernel, plan),
        out_shape=(
            square, square, square, square,
            jax.ShapeDtypeStruct((1, w), F32),
            jax.ShapeDtypeStruct((1, w), F32),
            jax.ShapeDtypeStruct((plan.heads, plan.buckets), F32),
            jax.ShapeDtypeStruct((plan.experts, w), F32),
            jax.ShapeDtypeStruct((2, plan.experts), jnp.int32),
        ),
        grid=(plan.lanes,),
        in_specs=[
            pl.BlockSpec((1, w, 128), lambda i: (0, i, 0)), spec(0), spec(1), spec(2),
            whole(small.shape),
        ],
        out_specs=(
            column, column, column, column,
            whole((1, w)), whole((1, w)), whole((plan.heads, plan.buckets)),
            whole((plan.experts, w)), whole((2, plan.experts)),
        ),
        compiler_params=pltpu.CompilerParams(vmem_limit_bytes=32 * MIB),
        name="weight_grad_layout",
    )(flat, flat, flat, flat, small)


def per_device(
    plan, inputs, segments, expert_index, gain_attn, query_weight, key_weight, value_weight, output_weight,
    bias_table, gain_ffn, router_weight, expert_in, expert_out, cotangent,
):
    eidx = expert_index.reshape(1, plan.tokens)
    g1, g2 = gain_attn.reshape(1, plan.width), gain_ffn.reshape(1, plan.width)
    router = router_weight.T
    (ct_rows, routed_rows, e, rinv, normed, q, k, v, mixed, hidden, aux) = forward_part(
        plan, inputs, segments, eidx, g1, query_weight, key_weight, value_weight, output_weight,
        bias_table.T, g2, router, cotangent,
    )
    home, ret, rows, gret, act, gi, rgrad = expert_part(
        plan, routed_rows, ct_rows, expert_in, expert_out, router
    )
    expert_in_grad, expert_out_grad = weight_grads(plan, rows, gret, act, gi)
    output, input_grad, flat, small, _ = backward_part(
        plan, home, ret, e, rinv, normed, q, k, v, mixed, hidden, aux, eidx, inputs, cotangent,
        query_weight, key_weight, value_weight, output_weight, g1, g2, rgrad,
    )
    out_grad, q_grad, k_grad, v_grad, gain1, gain2, table, router_grad, counts = finish_part(
        plan, flat, small
    )
    return (
        output, input_grad, gain1.reshape(-1), q_grad, k_grad, v_grad, out_grad, table.T,
        gain2.reshape(-1), router_grad.T, expert_in_grad, expert_out_grad, counts,
    )


def solution(mesh):
    split = P(AXES, None)
    cube = P(AXES, None, None)
    n_local = mesh.shape["local"]
    n = mesh.shape["group"] * n_local

    def run(*args):
        tokens, width = args[0].shape
        buckets, heads = args[8].shape
        plan = Plan(n, n_local, tokens, width, args[10].shape[1], heads, buckets)
        return per_device(plan, *args)

    return jax.shard_map(
        run,
        mesh=mesh,
        in_specs=(split, split, split) + (P(),) * 8 + (cube, cube, split),
        out_specs=(split, split) + (P(),) * 8 + (cube, cube, P()),
        check_vma=False,
    )
```

```python
import functools

import jax
import jax.numpy as jnp
from jax import lax
from jax.experimental import pallas as pl
from jax.experimental.pallas import tpu as pltpu
from jax.sharding import PartitionSpec as P

MESH = pl.DeviceIdType.MESH
AXES = ("group", "local")
epsilon = 1e-06
score_scale = 0.125
masked_score = -1000000000.0
far_limits = (12, 16, 23, 32, 46, 64, 91)
MIB = 2**20
BF = jnp.bfloat16
F32 = jnp.float32


def nn(a, b):
    return jnp.dot(a, b, preferred_element_type=F32)


def nt(a, b):
    return lax.dot_general(a, b, (((1,), (1,)), ((), ())), preferred_element_type=F32)


def tn(a, b):
    return lax.dot_general(a, b, (((0,), (0,)), ((), ())), preferred_element_type=F32)


def iota(shape, dim):
    return lax.broadcasted_iota(jnp.int32, shape, dim)


class Plan:
    def __init__(self, n, n_local, tokens, width, experts, heads, buckets):
        self.n, self.n_local, self.tokens, self.width = n, n_local, tokens, width
        self.experts, self.heads, self.buckets = experts, heads, buckets
        self.head = width // heads
        self.cap = (5 * tokens + 4 * experts - 1) // (4 * experts)
        self.lanes = width // 128
        self.folded = 16 < self.cap <= 20 and self.lanes == 6
        self.rows = 16 if self.folded else -(-self.cap // 16) * 16
        self.packed = width + 256 if self.folded else width
        self.slots = n * self.rows
        self.extra = n * 4 if self.folded else 0

    def peer(self, me, k):
        c = (me % 2 + k % 2) % 2
        x = ((me // 2) % 2 + (k // 2) % 2) % 2
        y = ((me // 4) % 2 + (k // 4) % 2) % 2
        return self.plane_at(me // 8, k // 8) * 8 + y * 4 + x * 2 + c

    def plane_at(self, z, k):
        depth = self.n // 8
        return ((z // 2 + k // 2) % (depth // 2)) * 2 + (z % 2 + k % 2) % 2

    def plane_back(self, k):
        depth = self.n // 8
        return ((depth // 2 - k // 2) % (depth // 2)) * 2 + k % 2

    def coords(self, d):
        return (d // self.n_local, d % self.n_local)


def me_index(plan):
    return lax.axis_index("group") * plan.n_local + lax.axis_index("local")


def greet_all(plan, me):
    barrier = pltpu.get_barrier_semaphore()

    def one(k, carry):
        pl.semaphore_signal(
            barrier, inc=1, device_id=plan.coords(plan.peer(me, k)), device_id_type=MESH
        )
        return carry

    lax.fori_loop(1, plan.n, one, 0)
    return lambda: pl.semaphore_wait(barrier, plan.n - 1)


def block_copy(plan, me, k, src, dst, send_sem, recv_sem):
    target = plan.peer(me, k)
    rows = plan.rows
    return pltpu.make_async_remote_copy(
        src_ref=src.at[pl.ds(pl.multiple_of(target * rows, rows), rows), :],
        dst_ref=dst.at[pl.ds(pl.multiple_of(me * rows, rows), rows), :],
        send_sem=send_sem.at[k],
        recv_sem=recv_sem.at[k],
        device_id=plan.coords(target),
        device_id_type=MESH,
    )


def own_copy(plan, me, src, dst, sem):
    rows = plan.rows
    place = pl.ds(pl.multiple_of(me * rows, rows), rows)
    return pltpu.make_async_copy(src.at[place, :], dst.at[place, :], sem)


def start_all(plan, me, src, dst, send_sem, recv_sem):
    half = plan.n // 2

    def one(i, carry):
        block_copy(plan, me, half + i, src, dst, send_sem, recv_sem).start()
        block_copy(plan, me, i, src, dst, send_sem, recv_sem).start()
        return carry

    block_copy(plan, me, half, src, dst, send_sem, recv_sem).start()
    lax.fori_loop(1, half, one, 0)
    own_copy(plan, me, src, dst, send_sem.at[0]).start()


def wait_all(plan, me, src, dst, send_sem, recv_sem):
    def one(k, carry):
        block_copy(plan, me, k, src, dst, send_sem, recv_sem).wait()
        return carry

    lax.fori_loop(1, plan.n, one, 0)
    own_copy(plan, me, src, dst, send_sem.at[0]).wait()


def slot_rows(plan, ids):
    for at in range(0, plan.slots, 512):
        size = min(512, plan.slots - at)
        place = iota((size, plan.tokens), 0) + at
        main = jnp.where(place.astype(F32) == ids[1:2, :], 1.0, 0.0).astype(BF)
        extra = None
        if plan.folded:
            folded = ((place // 16) * 4 + place % 4).astype(F32)
            extra = jnp.where(folded == ids[2:3, :], 1.0, 0.0).astype(BF)
        yield at, size, main, extra


def fold(plan, full, count):
    part = (iota((count, 128), 0) % 16) // 4
    first = jnp.where(part == 0, full[:, 0:128], 0.0)
    for g in range(1, 4):
        first = jnp.where(part == g, full[:, 128 * g : 128 * g + 128], first)
    second = jnp.where(part == 0, full[:, 512:640], jnp.where(part == 1, full[:, 640:768], 0.0))
    return first, second


def dispatch_to(plan, blocks, values, out_ref):
    for at, size, main, extra in blocks:
        rows = slice(at, at + size)
        out_ref[rows, 0 : plan.width] = nn(main, values).astype(BF)
        if plan.folded:
            first, second = fold(plan, nn(extra, values), size)
            out_ref[rows, 768:896] = first.astype(BF)
            out_ref[rows, 896:1024] = second.astype(BF)


def token_slots(plan, eidx_row):
    t, e = plan.tokens, plan.experts
    pick = jnp.where(eidx_row == iota((e, t), 0), 1.0, 0.0)
    upper = jnp.where(iota((t, t), 0) <= iota((t, t), 1), 1.0, 0.0).astype(BF)
    running = nn(pick.astype(BF), upper)
    position = jnp.sum(running * pick, axis=0, keepdims=True) - 1.0
    chosen = eidx_row.astype(F32)
    if plan.folded:
        main = jnp.where(position < 16.0, chosen * 16.0 + position, -1.0)
        extra = jnp.where(
            (position >= 16.0) & (position < plan.cap), chosen * 4.0 + (position - 16.0), -1.0
        )
    else:
        main = jnp.where(position < plan.cap, chosen * float(plan.rows) + position, -1.0)
        extra = jnp.full_like(main, -1.0)
    row = iota((128, t), 0)
    return jnp.where(
        row == 1, main, jnp.where(row == 2, extra, jnp.where(row == 3, chosen, 0.0))
    )


def bucket_rows(shape, offset):
    distance = jnp.abs(offset)
    far = jnp.zeros(shape, jnp.int32) + 8
    for threshold in far_limits:
        far = far + (distance >= threshold).astype(jnp.int32)
    return jnp.where(distance < 8, distance, far) + 16 * (offset > 0).astype(jnp.int32)


def bucket_onehot(buckets, span):
    lane = iota((buckets, span), 1)
    signed = jnp.where(lane < 896, 384 - lane, 384 + span - lane)
    return jnp.where(bucket_rows((buckets, span), signed) == iota((buckets, span), 0), 1.0, 0.0)


def rms(values):
    return lax.rsqrt(jnp.mean(values * values, axis=-1, keepdims=True) + epsilon)


SPAN = 1024


def unfold_picks(count, g):
    row = iota((count // 4, count), 0)
    place = (row // 4) * 16 + g * 4 + row % 4
    return jnp.where(iota((count // 4, count), 1) == place, 1.0, 0.0).astype(BF)


def unfold(lanes, count):
    parts = [nn(unfold_picks(count, g), lanes) for g in range(4)]
    return jnp.concatenate(
        [parts[0][:, 0:128], parts[1][:, 0:128], parts[2][:, 0:128], parts[3][:, 0:128],
         parts[0][:, 128:256], parts[1][:, 128:256]],
        axis=1,
    ).astype(BF)


def refold(plan, rows, count):
    row = iota((count, count // 4), 0)
    place = (row // 16) * 4 + row % 4
    picks = jnp.where(iota((count, count // 4), 1) == place, 1.0, 0.0).astype(BF)
    return fold(plan, nn(picks, rows), count)


def forward_kernel(
    plan, groups,
    x_ref, seg_ref, eidx_ref, g1_ref, wq_hbm, wk_hbm, wv_hbm, wo_hbm, table_ref, g2_ref, rw_ref, ct_ref, w1_hbm, w2_hbm,
    home_out, e_out, normed_hbm, q_hbm, k_hbm, v_hbm, mixed_hbm, hidden_hbm, act_out, gi_out, ret_out,
    rinv_out, aux_out, rows_out, gret_out, rgrad_out,
    wq_ref, wk_ref, wv_ref, wo_ref, w1, w2, normed_out, q_out, k_out, v_out, mixed_out, hidden_out,
    ct_send, ct_recv, routed_send, land, pool, mask, s_buf, e_buf, vt, act, gi, gl_all,
    ct_sent, ct_come, send_sem, recv_sem, back_send, back_recv, load_sem, save_sem, e_sem, out_sem,
):
    t = plan.tokens
    me = me_index(plan)
    everyone = greet_all(plan, me)
    loads = [
        pltpu.make_async_copy(src, dst, load_sem.at[i])
        for i, (src, dst) in enumerate(
            ((wq_hbm, wq_ref), (wk_hbm, wk_ref), (wv_hbm, wv_ref), (wo_hbm, wo_ref),
             (w1_hbm.at[0], w1), (w2_hbm.at[0], w2))
        )
    ]
    for load in loads:
        load.start()

    def save(i):
        src, dst = (
            (normed_out, normed_hbm), (q_out, q_hbm), (k_out, k_hbm), (v_out, v_hbm), (mixed_out, mixed_hbm),
            (hidden_out, hidden_hbm),
        )[i]
        return pltpu.make_async_copy(src, dst, save_sem.at[i])

    ids = token_slots(plan, eidx_ref[...])
    places = list(slot_rows(plan, ids)) if plan.folded else None
    dispatch_to(plan, places or slot_rows(plan, ids), ct_ref[...], ct_send)
    everyone()
    start_all(plan, me, ct_send, ct_recv, ct_sent, ct_come)

    tokens = x_ref[...].astype(F32)
    normed = (tokens * rms(tokens) * g1_ref[...].reshape(1, plan.width)).astype(BF)
    normed_out[...] = normed
    save(0).start()
    for load in loads[0:3]:
        load.wait()
    q_out[...] = (nn(normed, wq_ref[...]).astype(BF).astype(F32) * score_scale).astype(BF)
    k_out[...] = nn(normed, wk_ref[...]).astype(BF)
    v_out[...] = nn(normed, wv_ref[...]).astype(BF)
    for i in (1, 2, 3):
        save(i).start()
    vt[...] = v_out[...].T

    base = jnp.dot(
        table_ref[...],
        bucket_onehot(plan.buckets, SPAN),
        precision=lax.Precision.HIGHEST,
        preferred_element_type=F32,
    )
    for h in range(plan.heads):
        row = jnp.broadcast_to(base[h : h + 1, :], (128, SPAN))
        pool[128 * h : 128 * h + 128, :] = pltpu.roll(row, 0, 1, stride=1, stride_axis=0)
    seg_row = seg_ref[...].astype(F32)
    seg_col = jnp.broadcast_to(seg_row, (128, t)).T[:, 0:1]
    mask[...] = jnp.where(seg_col == seg_row, 0.0, masked_score)

    def pair(p, carry):
        lanes = pl.ds(pl.multiple_of(p * 128, 128), 128)
        for side in range(2):
            h = 2 * p + side
            keep = (iota((t, 128), 1) // 64) == side
            qm = jnp.where(keep, q_out[:, lanes], jnp.zeros((), BF))
            for ib in range(t // 256):
                cols = slice(256 * ib, 256 * ib + 256)
                top = jnp.full((8, 256), -3.0e38, F32)
                for jb in range(t // 128):
                    rows = slice(128 * jb, 128 * jb + 128)
                    start = 384 - 128 * jb + 256 * ib
                    s = nt(k_out[rows, lanes], qm[cols, :])
                    s = s + pool[pl.ds(pl.multiple_of(h * 128, 128), 128), start : start + 256] + mask[rows, cols]
                    s_buf[rows, cols] = s
                    top = jnp.maximum(top, jnp.max(s.reshape(16, 8, 256), axis=0))
                top = jnp.max(top, axis=0, keepdims=True)
                total = jnp.zeros((8, 256), F32)
                for jb in range(t // 128):
                    rows = slice(128 * jb, 128 * jb + 128)
                    ex = jnp.exp(s_buf[rows, cols] - top)
                    e_buf[h, rows, cols] = ex.astype(BF)
                    total = total + jnp.sum(ex.reshape(16, 8, 256), axis=0)
                rinv_out[pl.ds(h, 1), cols] = 1.0 / jnp.sum(total, axis=0, keepdims=True)
            pltpu.make_async_copy(e_buf.at[h], e_out.at[h], e_sem.at[h]).start()
            place = pl.ds(pl.multiple_of(p * 128 + side * 64, 64), 64)
            mixed = nn(vt[place, :], e_buf[h]) * rinv_out[pl.ds(h, 1), :]
            vt[place, :] = mixed.astype(BF)
        return carry

    lax.fori_loop(0, plan.heads // 2, pair, 0)
    mixed_out[...] = vt[...].T
    save(4).start()
    loads[3].wait()
    hidden = tokens + nn(mixed_out[...], wo_ref[...])
    hidden_out[...] = hidden
    save(5).start()
    routed = (hidden * rms(hidden) * g2_ref[...].reshape(1, plan.width)).astype(BF)
    logits = nt(routed, rw_ref[...])
    grown = jnp.exp(logits - jnp.max(logits, axis=1, keepdims=True))
    probs = grown / jnp.sum(grown, axis=1, keepdims=True)
    columns = ids.T
    pick = columns[:, 3:4] == iota((t, plan.experts), 1).astype(F32)
    gate = jnp.sum(jnp.where(pick, probs, 0.0), axis=1, keepdims=True)
    aux_out[...] = jnp.where(iota((t, 128), 1) == 0, gate, columns)
    dispatch_to(plan, places or slot_rows(plan, ids), routed, routed_send)


    planes = plan.n // 8
    main_rows = 8 * plan.rows
    plane_rows = main_rows + (32 if plan.folded else 0)
    z = me // 8
    ff = w1.shape[1]
    step = 512

    start_all(plan, me, routed_send, land, send_sem, recv_sem)
    own_copy(plan, me, ct_send, ct_recv, ct_sent.at[0]).wait()

    def keep(number, i):
        rows = len(groups[number]) * plane_rows
        src, dst = ((act, act_out), (gi, gi_out))[i]
        return pltpu.make_async_copy(
            src.at[0:rows, :], dst.at[pl.ds(groups[number][0] * plane_rows, rows), :], out_sem.at[2 * number + i]
        )

    def place_of(kz):
        source = plan.plane_at(z, plan.plane_back(kz))
        return pl.ds(pl.multiple_of(source * main_rows, main_rows), main_rows)

    def assemble(kz, packed, target):
        base = kz * plane_rows
        place = place_of(kz)
        target[base : base + main_rows, :] = packed[place, 0 : plan.width]
        if plan.folded:
            target[base + main_rows : base + plane_rows, :] = unfold(
                packed[place, 768:1024], main_rows
            )

    def pack(kz, values, target):
        place = place_of(kz)
        target[place, 0 : plan.width] = values[0:main_rows, :]
        if plan.folded:
            first, second = refold(plan, values[main_rows:plane_rows, :], main_rows)
            target[place, 768:896] = first.astype(BF)
            target[place, 896:1024] = second.astype(BF)

    for number, members in enumerate(groups):
        group = len(members) * plane_rows
        for kz in members:
            if kz == 0:
                own_copy(plan, me, routed_send, land, send_sem.at[0]).wait()
            def arrived(low, carry, kz=kz):
                block_copy(plan, me, kz * 8 + low, ct_send, ct_recv, ct_sent, ct_come).wait_recv()
                block_copy(plan, me, kz * 8 + low, routed_send, land, send_sem, recv_sem).wait_recv()
                return carry
            lax.fori_loop(1 if kz == 0 else 0, 8, arrived, 0)
            assemble(kz, land, rows_out)
            assemble(kz, ct_recv, gret_out)
        if number == 0:
            def gone(k, carry):
                block_copy(plan, me, k, ct_send, ct_recv, ct_sent, ct_come).wait_send()
                return carry
            lax.fori_loop(1, plan.n, gone, 0)
            loads[4].wait()
            loads[5].wait()
        mine = slice(members[0] * plane_rows, members[0] * plane_rows + group)
        rows = rows_out[mine, :]
        raw = gret_out[mine, :]
        logits = nt(rows, rw_ref[...])
        grown = jnp.exp(logits - jnp.max(logits, axis=1, keepdims=True))
        probs = grown / jnp.sum(grown, axis=1, keepdims=True)
        chosen = jnp.where(iota((group, plan.experts), 1) == me, 1.0, 0.0)
        gate = jnp.sum(probs * chosen, axis=1, keepdims=True)
        gret_out[mine, :] = (gate * raw.astype(F32)).astype(BF)
        if number > 0:
            for i in (0, 1):
                keep(number - 1, i).wait()
        for at in range(0, ff, step):
            cols = slice(at, at + step)
            inner = nn(rows_out[mine, :], w1[:, cols])
            grad = nt(gret_out[mine, :], w2[cols, :])
            square = inner * inner
            slope = 0.7978845608028654 + 0.1070322244 * square
            tanh = jnp.tanh(inner * (0.7978845608028654 + 0.035677408136300125 * square))
            half = 0.5 + 0.5 * tanh
            act[0:group, cols] = (inner * half).astype(BF)
            gi[0:group, cols] = (grad * (half + 0.5 * inner * (1.0 - tanh * tanh) * slope)).astype(BF)
            if at == 0:
                pool[0:group, 0:768] = nn(act[0:group, cols], w2[cols, :])
                pool[group : 2 * group, 0:768] = nt(gi[0:group, cols], w1[:, cols])
            else:
                pool[0:group, 0:768] += nn(act[0:group, cols], w2[cols, :])
                pool[group : 2 * group, 0:768] += nt(gi[0:group, cols], w1[:, cols])
        answer = pool[0:group, 0:768].astype(BF)
        grad_gate = jnp.sum(raw.astype(F32) * answer.astype(F32), axis=1, keepdims=True)
        grad_logits = (probs * (chosen - gate) * grad_gate).astype(BF)
        gl_all[mine, :] = grad_logits
        back = (pool[group : 2 * group, 0:768] + nn(grad_logits, rw_ref[...])).astype(BF)
        for at, kz in enumerate(members):
            part = slice(at * plane_rows, (at + 1) * plane_rows)
            pack(kz, back[part, :], ct_send)
            if kz == 0:
                own_copy(plan, me, ct_send, home_out, back_send.at[0]).start()
            def send(low, carry, kz=kz):
                k = plan.plane_back(kz) * 8 + low
                block_copy(plan, me, k, ct_send, home_out, back_send, back_recv).start()
                return carry
            lax.fori_loop(1 if kz == 0 else 0, 8, send, 0)
            pack(kz, answer[part, :], land)
        for i in (0, 1):
            keep(number, i).start()
    give_back = pltpu.make_async_copy(land, ret_out, save_sem.at[6])
    give_back.start()
    rgrad_out[...] = tn(gl_all[...], rows_out[...])
    for i in (0, 1):
        keep(len(groups) - 1, i).wait()
    for i in range(6):
        save(i).wait()
    give_back.wait()

    def drain(h, carry):
        pltpu.make_async_copy(e_buf.at[h], e_out.at[h], e_sem.at[h]).wait()
        return carry

    lax.fori_loop(0, plan.heads, drain, 0)

    def sent(k, carry):
        block_copy(plan, me, k, routed_send, land, send_sem, recv_sem).wait_send()
        return carry

    lax.fori_loop(1, plan.n, sent, 0)
    wait_all(plan, me, ct_send, home_out, back_send, back_recv)


def forward_part(plan, x, seg, eidx, g1, wq, wk, wv, wo, table, g2, rw, ct, w1, w2):
    planes = plan.n // 8
    groups = ((2,), (0, 1), (3,)) if planes == 4 else tuple((kz,) for kz in range(planes))
    total = plan.slots + plan.extra
    group = max(len(members) for members in groups) * total // planes
    t, w, h, n, e, ff = plan.tokens, plan.width, plan.heads, plan.n, plan.experts, w1.shape[2]
    block = jax.ShapeDtypeStruct((plan.slots, plan.packed), BF)
    state = jax.ShapeDtypeStruct((t, w), BF)
    vmem = pl.BlockSpec(memory_space=pltpu.VMEM)
    any_ = pl.BlockSpec(memory_space=pl.ANY)
    packed = pltpu.VMEM((plan.slots, plan.packed), BF)
    rows = pltpu.VMEM((t, w), BF)
    weight = pltpu.VMEM((w, w), BF)
    each = pltpu.SemaphoreType.DMA((n,))
    return pl.pallas_call(
        functools.partial(forward_kernel, plan, groups),
        out_shape=(
            block,
            jax.ShapeDtypeStruct((h, t, t), BF),
            state, state, state, state, state,
            jax.ShapeDtypeStruct((t, w), F32),
            jax.ShapeDtypeStruct((total, ff), BF),
            jax.ShapeDtypeStruct((total, ff), BF),
            block,
            jax.ShapeDtypeStruct((16, t), F32),
            jax.ShapeDtypeStruct((t, 128), F32),
            jax.ShapeDtypeStruct((total, w), BF),
            jax.ShapeDtypeStruct((total, w), BF),
            jax.ShapeDtypeStruct((e, w), F32),
        ),
        in_specs=[vmem] * 4 + [any_] * 4 + [vmem] * 4 + [any_] * 2,
        out_specs=(any_,) * 11 + (vmem,) * 5,
        scratch_shapes=[
            weight, weight, weight, weight,
            pltpu.VMEM((w, ff), BF),
            pltpu.VMEM((ff, w), BF),
            rows, rows, rows, rows, rows,
            pltpu.VMEM((t, w), F32),
            packed, packed, packed, packed,
            pltpu.VMEM((max(h * 128, 2 * group), SPAN), F32),
            pltpu.VMEM((t, t), F32),
            pltpu.VMEM((t, t), F32),
            pltpu.VMEM((h, t, t), BF),
            pltpu.VMEM((w, t), BF),
            pltpu.VMEM((group, ff), BF),
            pltpu.VMEM((group, ff), BF),
            pltpu.VMEM((total, e), BF),
            each, each, each, each, each, each,
            pltpu.SemaphoreType.DMA((6,)),
            pltpu.SemaphoreType.DMA((7,)),
            pltpu.SemaphoreType.DMA((h,)),
            pltpu.SemaphoreType.DMA((2 * planes,)),
        ],
        compiler_params=pltpu.CompilerParams(
            collective_id=0, has_side_effects=True, vmem_limit_bytes=(60 if n == 32 else 63) * MIB
        ),
        name="forward_and_experts",
    )(x, seg, eidx, g1, wq, wk, wv, wo, table, g2, rw, ct, w1, w2)


class Reducer:
    STEPS = 10

    def __init__(self, plan, me, src, near, mid, far, near_stage, mid_stage, out, sems, slot):
        self.plan, self.me, self.src, self.out = plan, me, src, out
        self.near, self.mid, self.far = near, mid, far
        self.near_stage, self.mid_stage = near_stage, mid_stage
        self.sems, self.slot = sems, slot
        rows = src.shape[0]
        self.half, self.quarter, self.own = rows // 2, rows // 8, rows // plan.n
        self.piece = self.quarter // 2
        self.depth = plan.n // 8
        self.core, self.x, self.y, self.z = me % 2, (me // 2) % 2, (me // 4) % 2, me // 8
        self.half_at = self.core * self.half

    def span(self, start, size):
        return pl.ds(pl.multiple_of(start, self.own), size)

    def quarter_of(self, x, y):
        return self.half_at + (2 * y + x) * self.quarter

    def remote(self, src, dst, place, k):
        send, recv = self.sems
        return pltpu.make_async_remote_copy(
            src_ref=src, dst_ref=dst,
            send_sem=send.at[self.slot, place], recv_sem=recv.at[self.slot, place],
            device_id=self.plan.coords(self.plan.peer(self.me, k)), device_id_type=MESH,
        )

    def cross(self):
        away = self.span((1 - self.core) * self.half, self.half)
        return [self.remote(self.src.at[away, :], self.near, 0, 1)]

    def plane(self):
        copies = []
        for o, (x, y) in enumerate(((1 - self.x, self.y), (self.x, 1 - self.y), (1 - self.x, 1 - self.y))):
            at = self.span(self.quarter_of(x, y), self.quarter)
            copies.append(self.remote(self.src.at[at, :], self.mid.at[o], 1 + o, 2 * (o + 1)))
        return copies

    def along(self):
        at = self.quarter_of(self.x, self.y)
        return [
            self.remote(
                self.src.at[self.span(at + self.plan.plane_at(self.z, o) * self.own, self.own), :],
                self.far.at[o - 1], 11 + o, 8 * o,
            )
            for o in range(1, self.depth)
        ]

    def owned(self):
        return self.span(self.quarter_of(self.x, self.y) + self.z * self.own, self.own)

    def along_back(self):
        place = self.owned()
        return [
            self.remote(self.src.at[place, :], self.out.at[place, :], 11 + self.depth + o, 8 * o)
            for o in range(1, self.depth)
        ]

    def own_local(self):
        place = self.owned()
        return pltpu.make_async_copy(
            self.src.at[place, :], self.out.at[place, :], self.sems[0].at[self.slot, 11]
        )

    def again(self, at, size, place, k):
        where = self.span(at, size)
        return self.remote(self.out.at[where, :], self.out.at[where, :], place, k)

    def back_one(self):
        at = self.quarter_of(self.x, self.y)
        return [self.again(at, self.piece, 4, 2), self.again(at + self.piece, self.piece, 5, 4)]

    def back_two(self):
        at, size = self.quarter_of(self.x, self.y), self.piece
        return [
            self.again(at, size, 6, 4),
            self.again(self.quarter_of(1 - self.x, self.y), size, 7, 4),
            self.again(at + size, size, 8, 2),
            self.again(self.quarter_of(self.x, 1 - self.y) + size, size, 9, 2),
        ]

    def cross_back(self):
        return [self.again(self.half_at, self.half, 10, 1)]

    def fetch_near(self):
        return pltpu.make_async_copy(self.near, self.near_stage, self.sems[1].at[self.slot, 11])

    def fetch_mid(self):
        return pltpu.make_async_copy(self.mid, self.mid_stage, self.sems[1].at[self.slot, 11])

    def add(self, at, size, parts):
        place = self.span(at, size)
        total = self.src[place, :].astype(F32)
        for part in parts:
            total = total + part.astype(F32)
        self.src[place, :] = total.astype(BF)

    def step(self, number):
        def start(copies):
            for c in copies:
                c.start()

        def wait(copies):
            for c in copies:
                c.wait()

        if number == 0:
            start(self.cross())
        elif number == 1:
            wait(self.cross())
            self.fetch_near().start()
        elif number == 2:
            self.fetch_near().wait()
            self.add(self.half_at, self.half, [self.near_stage[...]])
            start(self.plane())
        elif number == 3:
            wait(self.plane())
            self.fetch_mid().start()
        elif number == 4:
            self.fetch_mid().wait()
            self.add(self.quarter_of(self.x, self.y), self.quarter, [self.mid_stage[o] for o in range(3)])
            start(self.along())
        elif number == 5:
            wait(self.along())
            at = self.quarter_of(self.x, self.y) + self.z * self.own
            self.add(at, self.own, [self.far[o] for o in range(self.depth - 1)])
            self.own_local().start()
            start(self.along_back())
        elif number == 6:
            self.own_local().wait()
            wait(self.along_back())
            start(self.back_one())
        elif number == 7:
            wait(self.back_one())
            start(self.back_two())
        elif number == 8:
            wait(self.back_two())
            start(self.cross_back())
        else:
            wait(self.cross_back())


ATTN, TABLE, COUNTS, SMALL = 8, 16, 28, 32


def chunk_rows(plan):
    unit = 16 * plan.n
    square = plan.lanes * plan.width
    return [
        -(-rows // unit) * unit for rows in (square + plan.lanes * plan.experts, square, 4 * plan.width)
    ]


def diagonal_sums(block):
    size = 64
    while size >= 8:
        block = block[0:size, :] + pltpu.roll(block[size : 2 * size, :], SPAN - size, 1)
        size //= 2
    row = iota((8, SPAN), 0)
    for bit in (4, 2, 1):
        block = jnp.where((row // bit) % 2 == 1, pltpu.roll(block, SPAN - bit, 1), block)
    return jnp.sum(block, axis=0, keepdims=True)


def norm_back(values, scale, gain, grad):
    weighted = gain * grad
    inner = jnp.mean(weighted * values, axis=-1, keepdims=True)
    back = scale * weighted - values * (scale * scale * scale * inner)
    return back, jnp.sum(grad * values * scale, axis=0, keepdims=True)


class Small:
    def __init__(self, plan, me, mine, others, send, recv):
        self.plan, self.me, self.mine, self.others, self.send, self.recv = plan, me, mine, others, send, recv

    def copies(self, block, place, offsets, base):
        return [
            pltpu.make_async_remote_copy(
                src_ref=block.at[place], dst_ref=block.at[place],
                send_sem=self.send.at[base + i], recv_sem=self.recv.at[base + i],
                device_id=self.plan.coords(self.plan.peer(self.me, k)), device_id_type=MESH,
            )
            for i, k in enumerate(offsets)
        ]

    def plane(self):
        return self.copies(self.mine, self.me % 8, range(1, 8), 0)

    def along(self):
        return self.copies(self.others, self.me // 8, range(8, self.plan.n, 8), 7)

    def step(self, number):
        if number == 0:
            for c in self.plane():
                c.start()
        elif number == 1:
            for c in self.plane():
                c.wait()
            total = self.mine[0]
            for i in range(1, 8):
                total = total + self.mine[i]
            self.others[self.me // 8] = total
            for c in self.along():
                c.start()
        else:
            for c in self.along():
                c.wait()

    def total(self):
        total = self.others[0]
        for i in range(1, self.plan.n // 8):
            total = total + self.others[i]
        return total


def backward_kernel(
    plan, schedule, batches,
    home_ref, ret_ref, e_hbm, hidden_hbm, ct_hbm, mixed_hbm, wo_hbm, normed_hbm, v_hbm, q_hbm, k_hbm, wq_hbm, wk_hbm,
    wv_hbm, x_hbm, rinv_ref, aux_ref, eidx_ref, g1_ref, g2_ref, rgrad_ref,
    output_out, input_out, flat0_out, flat1_out, flatqk_out, small_out,
    near0_hbm, near1_hbm, nearqk_hbm, mid0_hbm, mid1_hbm, midqk_hbm,
    hidden_ref, ct_ref, mixed_ref, wo_ref, normed_ref, v_ref, q_ref, k_ref, wq_ref, wk_ref, wv_ref, x_ref,
    home, ret, e_buf, dp_buf, ds_buf, skew, diag, scaled, across, dqt, dq, dk, dv, grad_hidden,
    flat0, flat1, flatqk, near0, near1, nearqk, mid0, mid1, midqk, far0, far1, farqk, small_plane, small_all,
    send_sem, recv_sem, e_sem, home_sem, load_sem, ar_send, ar_recv, small_send, small_recv,
):
    t, w, e = plan.tokens, plan.width, plan.experts
    me = me_index(plan)
    load_home = pltpu.make_async_copy(home_ref, home, home_sem)
    load_home.start()

    def load_e(h):
        return pltpu.make_async_copy(e_hbm.at[h], e_buf.at[h], e_sem.at[h])

    everyone = greet_all(plan, me)
    HIDDEN, CT, MIXED, WO, NORMED, V, Q, K, WQ, WK, WV, X = range(12)
    loads = [
        pltpu.make_async_copy(src, dst, load_sem.at[i])
        for i, (src, dst) in enumerate(
            ((hidden_hbm, hidden_ref), (ct_hbm, ct_ref), (mixed_hbm, mixed_ref), (wo_hbm, wo_ref),
             (normed_hbm, normed_ref), (v_hbm, v_ref), (q_hbm, q_ref), (k_hbm, k_ref), (wq_hbm, wq_ref),
             (wk_hbm, wk_ref), (wv_hbm, wv_ref), (x_hbm, x_ref))
        )
    ]
    for i in (HIDDEN, CT, MIXED, WO, NORMED):
        loads[i].start()
    for h in range(plan.heads):
        load_e(h).start()
    for i in (V, Q, K, WQ, WK, WV, X):
        loads[i].start()
    everyone()

    sems = (ar_send, ar_recv)
    sums = [
        Reducer(plan, me, flat0, near0_hbm, mid0_hbm, far0, near0, mid0, flat0_out, sems, 0),
        Reducer(plan, me, flat1, near1_hbm, mid1_hbm, far1, near1, mid1, flat1_out, sems, 1),
    ] + [
        Reducer(plan, me, flatqk.at[c], nearqk_hbm.at[c], midqk_hbm.at[c], farqk.at[c], nearqk.at[c], midqk.at[c],
                flatqk_out.at[c], sems, 2 + c)
        for c in range(3)
    ]
    sums.append(Small(plan, me, small_plane, small_all, small_send, small_recv))

    def advance(moment):
        if moment in batches:
            first, last = batches[moment]
            first, last = first * plan.n // 32, last * plan.n // 32

            def send(k, carry):
                block_copy(plan, me, k, ret_ref, ret, send_sem, recv_sem).start()
                return carry

            lax.fori_loop(max(first, 1), last, send, 0)
            if first == 0:
                own_copy(plan, me, ret_ref, ret, send_sem.at[0]).start()
        for c, number in schedule.get(moment, ()):
            sums[c].step(number)

    advance("start")
    square = plan.lanes * w
    flat0[square + plan.lanes * e :, :] = jnp.zeros((flat0.shape[0] - square - plan.lanes * e, 128), BF)
    if flat1.shape[0] > square:
        flat1[square:, :] = jnp.zeros((flat1.shape[0] - square, 128), BF)
    if flatqk.shape[1] > 4 * w:
        for c in range(3):
            flatqk[c, 4 * w :, :] = jnp.zeros((flatqk.shape[1] - 4 * w, 128), BF)
    for g in range(plan.lanes):
        flat0[square + e * g : square + e * g + e, :] = rgrad_ref[:, 128 * g : 128 * g + 128].astype(BF)

    aux = aux_ref[...]
    gate = aux[:, 0:1]
    dmain = jnp.where(iota((t, plan.slots), 1).astype(F32) == aux[:, 1:2], 1.0, 0.0).astype(BF)
    if plan.folded:
        dextra = jnp.where(iota((t, plan.extra), 1).astype(F32) == aux[:, 2:3], 1.0, 0.0).astype(BF)

    def combine(packed):
        total = nn(dmain, packed[:, 0:w])
        if plan.folded:
            total = total + nn(dextra, unfold(packed[:, 768:1024], plan.slots))
        return total

    def put(target, group, part):
        target[group * w : group * w + w, :] = part[:, 0:128]
        target[group * w + w : group * w + 2 * w, :] = part[:, 128:256]

    loads[MIXED].wait()
    across[...] = mixed_ref[...].T
    loads[HIDDEN].wait()
    loads[CT].wait()
    load_home.wait()
    hidden = hidden_ref[...]
    back, gain_ffn = norm_back(hidden, rms(hidden), g2_ref[...].reshape(1, w), combine(home))
    grad_hidden[...] = ct_ref[...].astype(F32) + back
    attended = grad_hidden[...].astype(BF)
    for b in range(w // 256):
        put(flat0, 2 * b, nn(across[...], attended[:, 256 * b : 256 * b + 256]).astype(BF))
    advance("out")
    spread = jnp.where(iota((16, w), 1) // plan.head == iota((16, w), 0), 1.0, 0.0)
    shares = jnp.dot(
        rinv_ref[...].T, spread, precision=lax.Precision.HIGHEST, preferred_element_type=F32
    )
    loads[WO].wait()
    loads[NORMED].wait()
    scaled[...] = (nt(attended, wo_ref[...]).astype(BF).astype(F32) * shares).astype(BF)
    across[...] = normed_ref[...].T

    def masked(ref, lanes, side):
        keep = (iota((t, 128), 1) // 64) == side
        return jnp.where(keep, ref[:, lanes], jnp.zeros((), BF))

    for p in range(plan.heads // 2):
        lanes = slice(128 * p, 128 * p + 128)
        load_e(2 * p).wait()
        load_e(2 * p + 1).wait()
        dv[:, lanes] = (
            nn(e_buf[2 * p], masked(scaled, lanes, 0)) + nn(e_buf[2 * p + 1], masked(scaled, lanes, 1))
        ).astype(BF)
    for b in range(w // 256):
        put(flat1, 2 * b, nn(across[...], dv[:, 256 * b : 256 * b + 256]).astype(BF))
    advance("value")
    for i in (V, Q, K):
        loads[i].wait()
    dqt[...] = k_ref[...].T
    skew[:, t + 384 :] = jnp.zeros((128, SPAN - t - 384), F32)

    for p in range(plan.heads // 2):
        lanes = slice(128 * p, 128 * p + 128)
        dk_pair = jnp.zeros((t, 128), F32)
        for side in range(2):
            h = 2 * p + side
            dom = masked(scaled, lanes, side)
            qm = masked(q_ref, lanes, side)
            skew[:, 0 : t + 384] = jnp.zeros((128, t + 384), F32)
            for ib in range(t // 256):
                cols = slice(256 * ib, 256 * ib + 256)
                delta = jnp.zeros((8, 256), F32)
                for jb in range(t // 128):
                    rows = slice(128 * jb, 128 * jb + 128)
                    dp = nt(v_ref[rows, lanes], dom[cols, :])
                    dp_buf[rows, cols] = dp
                    prod = dp * e_buf[h, rows, cols].astype(F32)
                    delta = delta + jnp.sum(prod.reshape(16, 8, 256), axis=0)
                delta = jnp.sum(delta, axis=0, keepdims=True) * rinv_ref[h : h + 1, cols]
                for jb in range(t // 128):
                    rows = slice(128 * jb, 128 * jb + 128)
                    start = 384 - 128 * jb + 256 * ib
                    ds = e_buf[h, rows, cols].astype(F32) * (dp_buf[rows, cols] - delta)
                    ds_buf[rows, cols] = ds.astype(BF)
                    skew[:, start : start + 256] += ds
                advance((h, ib))
            dk_pair = dk_pair + nn(ds_buf[...], qm)
            place = slice(64 * h, 64 * h + 64)
            dqt[place, :] = (nn(dqt[place, :], ds_buf[...]) * score_scale).astype(BF)
            diag[h : h + 1, :] = diagonal_sums(skew[...])
            if side == 1:
                dk[:, lanes] = dk_pair.astype(BF)
                dq[:, lanes] = dqt[128 * p : 128 * p + 128, :].T
                if p % 2 == 1:
                    cols = slice(256 * (p // 2), 256 * (p // 2) + 256)
                    target = flatqk.at[p // 2]
                    put(target, 0, nn(across[...], dq[:, cols]).astype(BF))
                    put(target, 2, nn(across[...], dk[:, cols]).astype(BF))
            advance((h, 2))

    for i in (WQ, WK, WV, X):
        loads[i].wait()
    grad_normed = nt(dq[...], wq_ref[...]) + nt(dk[...], wk_ref[...]) + nt(dv[...], wv_ref[...])
    tokens = x_ref[...].astype(F32)
    back, gain_attn = norm_back(tokens, rms(tokens), g1_ref[...].reshape(1, w), grad_normed)
    input_out[...] = (grad_hidden[...] + back).astype(BF)

    small = jnp.zeros((SMALL, 128), F32)
    mine = me % 8
    small_plane[mine] = small
    for g in range(plan.lanes):
        lanes = slice(128 * g, 128 * g + 128)
        small_plane[mine, g : g + 1, :] = gain_ffn[:, lanes]
        small_plane[mine, ATTN + g : ATTN + g + 1, :] = gain_attn[:, lanes]
    sums_table = lax.dot_general(
        diag[0 : plan.heads, :], bucket_onehot(plan.buckets, SPAN), (((1,), (1,)), ((), ())),
        precision=lax.Precision.HIGHEST, preferred_element_type=F32,
    )
    small_plane[mine, TABLE : TABLE + plan.heads, 0 : plan.buckets] = sums_table
    pick = jnp.where(eidx_ref[...] == iota((e, t), 0), 1.0, 0.0).astype(BF)
    load = nt(jnp.ones((8, t), BF), pick)[0:1, :]
    kept = jnp.minimum(load, float(plan.cap))
    small_plane[mine, COUNTS : COUNTS + 1, 0:e] = kept
    small_plane[mine, COUNTS + 1 : COUNTS + 2, 0:e] = load - kept
    advance("small")

    wait_all(plan, me, ret_ref, ret, send_sem, recv_sem)
    output_out[...] = (hidden_ref[...] + gate * combine(ret)).astype(BF)
    advance("tail")
    small_out[...] = sums[5].total()


BATCHES = {'start': (16, 32), 'out': (8, 16), 'value': (0, 8)}
SCHEDULE = {
    'out': ((0, 0),),
    'value': ((1, 0),),
    (1, 1): ((0, 1),),
    (2, 2): ((0, 2), (1, 1)),
    (3, 2): ((2, 0), (1, 2)),
    (6, 0): ((2, 1),),
    (7, 0): ((0, 3), (2, 2)),
    (7, 2): ((3, 0), (0, 4)),
    (9, 2): ((1, 3),),
    (10, 0): ((3, 1),),
    (10, 2): ((0, 5), (1, 4), (3, 2)),
    (11, 0): ((2, 3),),
    (11, 2): ((4, 0), (2, 4)),
    'small': ((0, 6), (5, 0)),
    'tail': ((3, 3), (4, 1), (1, 5), (5, 1), (3, 4), (4, 2), (2, 5), (0, 7), (1, 6), (5, 2), (4, 3), (3, 5), (4, 4), (2, 6), (0, 8), (3, 6), (1, 7), (4, 5), (2, 7), (3, 7), (0, 9), (4, 6), (1, 8), (2, 8), (1, 9), (3, 8), (2, 9), (4, 7), (3, 9), (4, 8), (4, 9)),
}


def backward_part(plan, home, ret, e, rinv, normed, q, k, v, mixed, hidden, aux, eidx, x, ct, wq, wk, wv, wo, g1, g2, rgrad):
    t, w, h, n = plan.tokens, plan.width, plan.heads, plan.n
    r0, r1, rq = chunk_rows(plan)
    depth = n // 8
    places = 11 + 2 * depth
    vmem = pl.BlockSpec(memory_space=pltpu.VMEM)
    any_ = pl.BlockSpec(memory_space=pl.ANY)
    state = jax.ShapeDtypeStruct((t, w), BF)
    bf = lambda *shape: jax.ShapeDtypeStruct(shape, BF)
    rows, weight = pltpu.VMEM((t, w), BF), pltpu.VMEM((w, w), BF)
    return pl.pallas_call(
        functools.partial(backward_kernel, plan, SCHEDULE, BATCHES),
        out_shape=(
            state, state, bf(r0, 128), bf(r1, 128), bf(3, rq, 128),
            jax.ShapeDtypeStruct((SMALL, 128), F32),
            bf(r0 // 2, 128), bf(r1 // 2, 128), bf(3, rq // 2, 128),
            bf(3, r0 // 8, 128), bf(3, r1 // 8, 128), bf(3, 3, rq // 8, 128),
        ),
        in_specs=[any_] * 15 + [vmem] * 6,
        out_specs=(vmem, vmem, any_, any_, any_, vmem) + (any_,) * 6,
        scratch_shapes=[
            pltpu.VMEM((t, w), F32),
            rows, rows, weight, rows, rows, rows, rows, weight, weight, weight, rows,
            pltpu.VMEM((plan.slots, plan.packed), BF),
            pltpu.VMEM((plan.slots, plan.packed), BF),
            pltpu.VMEM((h, t, t), BF),
            pltpu.VMEM((t, t), F32),
            pltpu.VMEM((t, t), BF),
            pltpu.VMEM((128, SPAN), F32),
            pltpu.VMEM((16, SPAN), F32),
            pltpu.VMEM((t, w), BF),
            pltpu.VMEM((w, t), BF),
            pltpu.VMEM((w, t), BF),
            pltpu.VMEM((t, w), BF),
            pltpu.VMEM((t, w), BF),
            pltpu.VMEM((t, w), BF),
            pltpu.VMEM((t, w), F32),
            pltpu.VMEM((r0, 128), BF),
            pltpu.VMEM((r1, 128), BF),
            pltpu.VMEM((3, rq, 128), BF),
            pltpu.VMEM((r0 // 2, 128), BF),
            pltpu.VMEM((r1 // 2, 128), BF),
            pltpu.VMEM((3, rq // 2, 128), BF),
            pltpu.VMEM((3, r0 // 8, 128), BF),
            pltpu.VMEM((3, r1 // 8, 128), BF),
            pltpu.VMEM((3, 3, rq // 8, 128), BF),
            pltpu.VMEM((depth - 1, r0 // n, 128), BF),
            pltpu.VMEM((depth - 1, r1 // n, 128), BF),
            pltpu.VMEM((3, depth - 1, rq // n, 128), BF),
            pltpu.VMEM((8, SMALL, 128), F32),
            pltpu.VMEM((depth, SMALL, 128), F32),
            pltpu.SemaphoreType.DMA((n,)),
            pltpu.SemaphoreType.DMA((n,)),
            pltpu.SemaphoreType.DMA((h,)),
            pltpu.SemaphoreType.DMA,
            pltpu.SemaphoreType.DMA((12,)),
            pltpu.SemaphoreType.DMA((5, places)),
            pltpu.SemaphoreType.DMA((5, places)),
            pltpu.SemaphoreType.DMA((6 + depth,)),
            pltpu.SemaphoreType.DMA((6 + depth,)),
        ],
        compiler_params=pltpu.CompilerParams(
            collective_id=2, has_side_effects=True, vmem_limit_bytes=60 * MIB
        ),
        name="backward_attention",
    )(home, ret, e, hidden, ct, mixed, wo, normed, v, q, k, wq, wk, wv, x, rinv, aux, eidx, g1, g2, rgrad)


def finish_kernel(
    plan, step,
    rows_hbm, gret_hbm, act_hbm, gi_hbm, flat0_hbm, flat1_hbm, flatqk_hbm, output_hbm, input_hbm, small_ref,
    ein_out, eout_out, out_out, v_out, q_out, k_out, output_out, input_out, g1_ref, g2_ref, table_ref, rw_ref, counts_ref,
    rows, gret, act, gi, flat0, flat1, flatqk, turned, ein, eout, square, passing, in_sem, act_sem, gi_sem, ein_sem, eout_sem, out_sem,
):
    w, e = plan.width, plan.experts
    chunks, depth = act_hbm.shape[1] // step, act.shape[0]

    def cut(i):
        return pl.ds(i * step, step)

    load = [
        pltpu.make_async_copy(src, dst, in_sem.at[i])
        for i, (src, dst) in enumerate(
            ((rows_hbm, rows), (gret_hbm, gret), (flat0_hbm, flat0), (flat1_hbm, flat1), (flatqk_hbm, flatqk),
             (output_hbm, passing.at[0]), (input_hbm, passing.at[1]))
        )
    ]
    load_act = [pltpu.make_async_copy(act_hbm.at[:, cut(i)], act.at[i % depth], act_sem.at[i]) for i in range(chunks)]
    load_gi = [pltpu.make_async_copy(gi_hbm.at[:, cut(i)], gi.at[i % depth], gi_sem.at[i]) for i in range(chunks)]
    save_in = [pltpu.make_async_copy(ein.at[:, cut(i)], ein_out.at[0, :, cut(i)], ein_sem.at[i]) for i in range(chunks)]
    save_out = [pltpu.make_async_copy(eout.at[cut(i), :], eout_out.at[0, cut(i), :], eout_sem.at[i]) for i in range(chunks)]
    save = [
        pltpu.make_async_copy(src, dst, out_sem.at[i])
        for i, (src, dst) in enumerate(
            ((square.at[0], out_out), (square.at[1], v_out), (square.at[2], q_out), (square.at[3], k_out),
             (passing.at[0], output_out), (passing.at[1], input_out))
        )
    ]
    for i in (2, 0):
        load[i].start()
    load_gi[0].start()
    load[1].start()
    load_act[0].start()
    for i in (3, 4):
        load[i].start()
    for i in range(1, depth):
        load_gi[i].start()
        load_act[i].start()
    load[5].start()
    load[6].start()

    def lay(m, source, groups):
        for g, at in groups:
            square[m, :, 128 * g : 128 * g + 128] = source(at).astype(F32)
        save[m].start()

    load[2].wait()
    lay(0, lambda at: flat0[at : at + w, :], [(g, g * w) for g in range(plan.lanes)])
    for g in range(plan.lanes):
        lanes = slice(128 * g, 128 * g + 128)
        at = plan.lanes * w + e * g
        rw_ref[:, lanes] = flat0[at : at + e, :].astype(F32)
        g2_ref[lanes] = small_ref[g, :]
        g1_ref[lanes] = small_ref[ATTN + g, :]
    table_ref[...] = small_ref[TABLE : TABLE + plan.heads, 0 : plan.buckets]
    counts_ref[...] = small_ref[COUNTS : COUNTS + 2, 0:e].astype(jnp.int32)
    load[0].wait()
    turned[...] = rows[...].T
    load[1].wait()
    for i in range(chunks):
        cols = slice(i * step, i * step + step)
        load_gi[i].wait()
        ein[:, cols] = nn(turned[...], gi[i % depth])
        save_in[i].start()
        load_act[i].wait()
        eout[cols, :] = tn(act[i % depth], gret[...])
        save_out[i].start()
        if i + depth < chunks:
            load_gi[i + depth].start()
            load_act[i + depth].start()
        if i == 0:
            load[3].wait()
            lay(1, lambda at: flat1[at : at + w, :], [(g, g * w) for g in range(plan.lanes)])
        if i == 1:
            load[4].wait()
            lay(2, lambda at: flatqk[at[0], at[1] : at[1] + w, :], [(g, (g // 2, (g % 2) * w)) for g in range(plan.lanes)])
        if i == 2:
            lay(3, lambda at: flatqk[at[0], at[1] : at[1] + w, :], [(g, (g // 2, (2 + g % 2) * w)) for g in range(plan.lanes)])
    for i in (4, 5):
        load[i + 1].wait()
        save[i].start()
    for copy in save + save_in + save_out:
        copy.wait()


def finish_part(plan, rows, gret, act, gi, flat0, flat1, flatqk, small, output, input_grad):
    t, w, e = plan.tokens, plan.width, plan.experts
    total, ff = act.shape
    step = 512
    chunks = ff // step
    depth = chunks if total <= 1024 else 2
    square = jax.ShapeDtypeStruct((w, w), F32)
    state = jax.ShapeDtypeStruct((t, w), BF)
    vmem = pl.BlockSpec(memory_space=pltpu.VMEM)
    any_ = pl.BlockSpec(memory_space=pl.ANY)
    each = pltpu.SemaphoreType.DMA((chunks,))
    return pl.pallas_call(
        functools.partial(finish_kernel, plan, step),
        out_shape=(
            jax.ShapeDtypeStruct((1, w, ff), F32),
            jax.ShapeDtypeStruct((1, ff, w), F32),
            square, square, square, square, state, state,
            jax.ShapeDtypeStruct((w,), F32),
            jax.ShapeDtypeStruct((w,), F32),
            jax.ShapeDtypeStruct((plan.heads, plan.buckets), F32),
            jax.ShapeDtypeStruct((e, w), F32),
            jax.ShapeDtypeStruct((2, e), jnp.int32),
        ),
        in_specs=[any_] * 9 + [vmem],
        out_specs=(any_,) * 8 + (vmem,) * 5,
        scratch_shapes=[
            pltpu.VMEM((total, w), BF),
            pltpu.VMEM((total, w), BF),
            pltpu.VMEM((depth, total, step), BF),
            pltpu.VMEM((depth, total, step), BF),
            pltpu.VMEM(flat0.shape, BF),
            pltpu.VMEM(flat1.shape, BF),
            pltpu.VMEM(flatqk.shape, BF),
            pltpu.VMEM((w, total), BF),
            pltpu.VMEM((w, ff), F32),
            pltpu.VMEM((ff, w), F32),
            pltpu.VMEM((4, w, w), F32),
            pltpu.VMEM((2, t, w), BF),
            pltpu.SemaphoreType.DMA((7,)),
            each, each, each, each,
            pltpu.SemaphoreType.DMA((6,)),
        ],
        compiler_params=pltpu.CompilerParams(vmem_limit_bytes=60 * MIB),
        name="weight_grads",
    )(rows, gret, act, gi, flat0, flat1, flatqk, output, input_grad, small)


def per_device(
    plan, inputs, segments, expert_index, gain_attn, query_weight, key_weight, value_weight, output_weight,
    bias_table, gain_ffn, router_weight, expert_in, expert_out, cotangent,
):
    eidx = expert_index.reshape(1, plan.tokens)
    g1, g2 = gain_attn, gain_ffn
    router = router_weight.T
    (home, e, normed, q, k, v, mixed, hidden, act, gi, ret, rinv, aux, rows, gret, rgrad) = forward_part(
        plan, inputs, segments, eidx, g1, query_weight, key_weight, value_weight, output_weight,
        bias_table.T, g2, router, cotangent, expert_in, expert_out,
    )
    output, input_grad, flat0, flat1, flatqk, small = backward_part(
        plan, home, ret, e, rinv, normed, q, k, v, mixed, hidden, aux, eidx, inputs, cotangent,
        query_weight, key_weight, value_weight, output_weight, g1, g2, rgrad,
    )[0:6]
    (expert_in_grad, expert_out_grad, out_grad, v_grad, q_grad, k_grad, output, input_grad, gain1, gain2, table,
     router_grad, counts) = finish_part(
        plan, rows, gret, act, gi, flat0, flat1, flatqk, small, output, input_grad
    )
    return (
        output, input_grad, gain1, q_grad, k_grad, v_grad, out_grad, table.T,
        gain2, router_grad.T, expert_in_grad, expert_out_grad, counts,
    )


def solution(mesh):
    split = P(AXES, None)
    cube = P(AXES, None, None)
    n_local = mesh.shape["local"]
    n = mesh.shape["group"] * n_local

    def run(*args):
        tokens, width = args[0].shape
        buckets, heads = args[8].shape
        plan = Plan(n, n_local, tokens, width, args[10].shape[1], heads, buckets)
        return per_device(plan, *args)

    return jax.shard_map(
        run,
        mesh=mesh,
        in_specs=(split, split, split) + (P(),) * 8 + (cube, cube, split),
        out_specs=(split, split) + (P(),) * 8 + (cube, cube, P()),
        check_vma=False,
    )
```

```python
import functools

import jax
import jax.numpy as jnp
from jax import lax
from jax.experimental import pallas as pl
from jax.experimental.pallas import tpu as pltpu
from jax.sharding import PartitionSpec as P

MESH = pl.DeviceIdType.MESH
AXES = ("group", "local")
epsilon = 1e-06
score_scale = 0.125
masked_score = -1000000000.0
far_limits = (12, 16, 23, 32, 46, 64, 91)
MIB = 2**20
BF = jnp.bfloat16
F32 = jnp.float32


def nn(a, b):
    return jnp.dot(a, b, preferred_element_type=F32)


def nt(a, b):
    return lax.dot_general(a, b, (((1,), (1,)), ((), ())), preferred_element_type=F32)


def tn(a, b):
    return lax.dot_general(a, b, (((0,), (0,)), ((), ())), preferred_element_type=F32)


def iota(shape, dim):
    return lax.broadcasted_iota(jnp.int32, shape, dim)


class Plan:
    def __init__(self, n, n_local, tokens, width, experts, heads, buckets):
        self.n, self.n_local, self.tokens, self.width = n, n_local, tokens, width
        self.experts, self.heads, self.buckets = experts, heads, buckets
        self.head = width // heads
        self.cap = (5 * tokens + 4 * experts - 1) // (4 * experts)
        self.lanes = width // 128
        self.folded = 16 < self.cap <= 20 and self.lanes == 6
        self.rows = 16 if self.folded else -(-self.cap // 16) * 16
        self.packed = width + 256 if self.folded else width
        self.slots = n * self.rows
        self.extra = n * 4 if self.folded else 0

    def peer(self, me, k):
        c = (me % 2 + k % 2) % 2
        x = ((me // 2) % 2 + (k // 2) % 2) % 2
        y = ((me // 4) % 2 + (k // 4) % 2) % 2
        return self.plane_at(me // 8, k // 8) * 8 + y * 4 + x * 2 + c

    def plane_at(self, z, k):
        depth = self.n // 8
        return ((z // 2 + k // 2) % (depth // 2)) * 2 + (z % 2 + k % 2) % 2

    def plane_back(self, k):
        depth = self.n // 8
        return ((depth // 2 - k // 2) % (depth // 2)) * 2 + k % 2

    def coords(self, d):
        return (d // self.n_local, d % self.n_local)


def me_index(plan):
    return lax.axis_index("group") * plan.n_local + lax.axis_index("local")


def greet_all(plan, me):
    barrier = pltpu.get_barrier_semaphore()

    def one(k, carry):
        pl.semaphore_signal(
            barrier, inc=1, device_id=plan.coords(plan.peer(me, k)), device_id_type=MESH
        )
        return carry

    lax.fori_loop(1, plan.n, one, 0)
    return lambda: pl.semaphore_wait(barrier, plan.n - 1)


def block_copy(plan, me, k, src, dst, send_sem, recv_sem):
    target = plan.peer(me, k)
    rows = plan.rows
    return pltpu.make_async_remote_copy(
        src_ref=src.at[pl.ds(pl.multiple_of(target * rows, rows), rows), :],
        dst_ref=dst.at[pl.ds(pl.multiple_of(me * rows, rows), rows), :],
        send_sem=send_sem.at[k],
        recv_sem=recv_sem.at[k],
        device_id=plan.coords(target),
        device_id_type=MESH,
    )


def own_copy(plan, me, src, dst, sem):
    rows = plan.rows
    place = pl.ds(pl.multiple_of(me * rows, rows), rows)
    return pltpu.make_async_copy(src.at[place, :], dst.at[place, :], sem)


def start_all(plan, me, src, dst, send_sem, recv_sem):
    half = plan.n // 2

    def one(i, carry):
        block_copy(plan, me, half + i, src, dst, send_sem, recv_sem).start()
        block_copy(plan, me, i, src, dst, send_sem, recv_sem).start()
        return carry

    block_copy(plan, me, half, src, dst, send_sem, recv_sem).start()
    lax.fori_loop(1, half, one, 0)
    own_copy(plan, me, src, dst, send_sem.at[0]).start()


def wait_all(plan, me, src, dst, send_sem, recv_sem):
    def one(k, carry):
        block_copy(plan, me, k, src, dst, send_sem, recv_sem).wait()
        return carry

    lax.fori_loop(1, plan.n, one, 0)
    own_copy(plan, me, src, dst, send_sem.at[0]).wait()


def slot_rows(plan, ids):
    for at in range(0, plan.slots, 512):
        size = min(512, plan.slots - at)
        place = iota((size, plan.tokens), 0) + at
        main = jnp.where(place.astype(F32) == ids[1:2, :], 1.0, 0.0).astype(BF)
        extra = None
        if plan.folded:
            folded = ((place // 16) * 4 + place % 4).astype(F32)
            extra = jnp.where(folded == ids[2:3, :], 1.0, 0.0).astype(BF)
        yield at, size, main, extra


def fold(plan, full, count):
    part = (iota((count, 128), 0) % 16) // 4
    first = jnp.where(part == 0, full[:, 0:128], 0.0)
    for g in range(1, 4):
        first = jnp.where(part == g, full[:, 128 * g : 128 * g + 128], first)
    second = jnp.where(part == 0, full[:, 512:640], jnp.where(part == 1, full[:, 640:768], 0.0))
    return first, second


def dispatch_to(plan, blocks, values, out_ref):
    for at, size, main, extra in blocks:
        rows = slice(at, at + size)
        out_ref[rows, 0 : plan.width] = nn(main, values).astype(BF)
        if plan.folded:
            first, second = fold(plan, nn(extra, values), size)
            out_ref[rows, 768:896] = first.astype(BF)
            out_ref[rows, 896:1024] = second.astype(BF)


def token_slots(plan, eidx_row):
    t, e = plan.tokens, plan.experts
    pick = jnp.where(eidx_row == iota((e, t), 0), 1.0, 0.0)
    upper = jnp.where(iota((t, t), 0) <= iota((t, t), 1), 1.0, 0.0).astype(BF)
    running = nn(pick.astype(BF), upper)
    position = jnp.sum(running * pick, axis=0, keepdims=True) - 1.0
    chosen = eidx_row.astype(F32)
    if plan.folded:
        main = jnp.where(position < 16.0, chosen * 16.0 + position, -1.0)
        extra = jnp.where(
            (position >= 16.0) & (position < plan.cap), chosen * 4.0 + (position - 16.0), -1.0
        )
    else:
        main = jnp.where(position < plan.cap, chosen * float(plan.rows) + position, -1.0)
        extra = jnp.full_like(main, -1.0)
    row = iota((128, t), 0)
    return jnp.where(
        row == 1, main, jnp.where(row == 2, extra, jnp.where(row == 3, chosen, 0.0))
    )


def bucket_rows(shape, offset):
    distance = jnp.abs(offset)
    far = jnp.zeros(shape, jnp.int32) + 8
    for threshold in far_limits:
        far = far + (distance >= threshold).astype(jnp.int32)
    return jnp.where(distance < 8, distance, far) + 16 * (offset > 0).astype(jnp.int32)


def bucket_onehot(buckets, span):
    lane = iota((buckets, span), 1)
    signed = jnp.where(lane < 896, 384 - lane, 384 + span - lane)
    return jnp.where(bucket_rows((buckets, span), signed) == iota((buckets, span), 0), 1.0, 0.0)


def rms(values):
    return lax.rsqrt(jnp.mean(values * values, axis=-1, keepdims=True) + epsilon)


SPAN = 1024


def unfold_picks(count, g):
    row = iota((count // 4, count), 0)
    place = (row // 4) * 16 + g * 4 + row % 4
    return jnp.where(iota((count // 4, count), 1) == place, 1.0, 0.0).astype(BF)


def unfold(lanes, count):
    parts = [nn(unfold_picks(count, g), lanes) for g in range(4)]
    return jnp.concatenate(
        [parts[0][:, 0:128], parts[1][:, 0:128], parts[2][:, 0:128], parts[3][:, 0:128],
         parts[0][:, 128:256], parts[1][:, 128:256]],
        axis=1,
    ).astype(BF)


def refold(plan, rows, count):
    row = iota((count, count // 4), 0)
    place = (row // 16) * 4 + row % 4
    picks = jnp.where(iota((count, count // 4), 1) == place, 1.0, 0.0).astype(BF)
    return fold(plan, nn(picks, rows), count)


def forward_kernel(
    plan, groups,
    x_ref, seg_ref, eidx_ref, g1_ref, wq_hbm, wk_hbm, wv_hbm, wo_hbm, table_ref, g2_ref, rw_ref, ct_ref, w1_hbm, w2_hbm,
    home_out, e_out, normed_hbm, q_hbm, k_hbm, v_hbm, mixed_hbm, hidden_hbm, act_out, gi_out, ret_out,
    rinv_out, aux_out, rows_out, gret_out, rgrad_out,
    wq_ref, wk_ref, wv_ref, wo_ref, w1, w2, normed_out, q_out, k_out, v_out, mixed_out, hidden_out,
    ct_send, ct_recv, routed_send, land, pool, mask, s_buf, e_buf, vt, act, gi, gl_all,
    ct_sent, ct_come, send_sem, recv_sem, back_send, back_recv, load_sem, save_sem, e_sem, out_sem,
):
    t = plan.tokens
    me = me_index(plan)
    everyone = greet_all(plan, me)
    loads = [
        pltpu.make_async_copy(src, dst, load_sem.at[i])
        for i, (src, dst) in enumerate(
            ((wq_hbm, wq_ref), (wk_hbm, wk_ref), (wv_hbm, wv_ref), (wo_hbm, wo_ref),
             (w1_hbm.at[0], w1), (w2_hbm.at[0], w2))
        )
    ]
    for load in loads:
        load.start()

    def save(i):
        src, dst = (
            (normed_out, normed_hbm), (q_out, q_hbm), (k_out, k_hbm), (v_out, v_hbm), (mixed_out, mixed_hbm),
            (hidden_out, hidden_hbm),
        )[i]
        return pltpu.make_async_copy(src, dst, save_sem.at[i])

    ids = token_slots(plan, eidx_ref[...])
    places = list(slot_rows(plan, ids)) if plan.folded else None
    dispatch_to(plan, places or slot_rows(plan, ids), ct_ref[...], ct_send)
    everyone()
    start_all(plan, me, ct_send, ct_recv, ct_sent, ct_come)

    tokens = x_ref[...].astype(F32)
    normed = (tokens * rms(tokens) * g1_ref[...].reshape(1, plan.width)).astype(BF)
    normed_out[...] = normed
    save(0).start()
    for load in loads[0:3]:
        load.wait()
    q_out[...] = (nn(normed, wq_ref[...]).astype(BF).astype(F32) * score_scale).astype(BF)
    k_out[...] = nn(normed, wk_ref[...]).astype(BF)
    v_out[...] = nn(normed, wv_ref[...]).astype(BF)
    for i in (1, 2, 3):
        save(i).start()
    vt[...] = v_out[...].T

    base = jnp.dot(
        table_ref[...],
        bucket_onehot(plan.buckets, SPAN),
        precision=lax.Precision.HIGHEST,
        preferred_element_type=F32,
    )
    for h in range(plan.heads):
        row = jnp.broadcast_to(base[h : h + 1, :], (128, SPAN))
        pool[128 * h : 128 * h + 128, :] = pltpu.roll(row, 0, 1, stride=1, stride_axis=0)
    seg_row = seg_ref[...].astype(F32)
    seg_col = jnp.broadcast_to(seg_row, (128, t)).T[:, 0:1]
    mask[...] = jnp.where(seg_col == seg_row, 0.0, masked_score)

    def pair(p, carry):
        lanes = pl.ds(pl.multiple_of(p * 128, 128), 128)
        for side in range(2):
            h = 2 * p + side
            keep = (iota((t, 128), 1) // 64) == side
            qm = jnp.where(keep, q_out[:, lanes], jnp.zeros((), BF))
            for ib in range(t // 256):
                cols = slice(256 * ib, 256 * ib + 256)
                top = jnp.full((8, 256), -3.0e38, F32)
                for jb in range(t // 128):
                    rows = slice(128 * jb, 128 * jb + 128)
                    start = 384 - 128 * jb + 256 * ib
                    s = nt(k_out[rows, lanes], qm[cols, :])
                    s = s + pool[pl.ds(pl.multiple_of(h * 128, 128), 128), start : start + 256] + mask[rows, cols]
                    s_buf[rows, cols] = s
                    top = jnp.maximum(top, jnp.max(s.reshape(16, 8, 256), axis=0))
                top = jnp.max(top, axis=0, keepdims=True)
                total = jnp.zeros((8, 256), F32)
                for jb in range(t // 128):
                    rows = slice(128 * jb, 128 * jb + 128)
                    ex = jnp.exp(s_buf[rows, cols] - top)
                    e_buf[h, rows, cols] = ex.astype(BF)
                    total = total + jnp.sum(ex.reshape(16, 8, 256), axis=0)
                rinv_out[pl.ds(h, 1), cols] = 1.0 / jnp.sum(total, axis=0, keepdims=True)
            pltpu.make_async_copy(e_buf.at[h], e_out.at[h], e_sem.at[h]).start()
            place = pl.ds(pl.multiple_of(p * 128 + side * 64, 64), 64)
            mixed = nn(vt[place, :], e_buf[h]) * rinv_out[pl.ds(h, 1), :]
            vt[place, :] = mixed.astype(BF)
        return carry

    lax.fori_loop(0, plan.heads // 2, pair, 0)
    mixed_out[...] = vt[...].T
    save(4).start()
    loads[3].wait()
    hidden = tokens + nn(mixed_out[...], wo_ref[...])
    hidden_out[...] = hidden
    save(5).start()
    routed = (hidden * rms(hidden) * g2_ref[...].reshape(1, plan.width)).astype(BF)
    logits = nt(routed, rw_ref[...])
    grown = jnp.exp(logits - jnp.max(logits, axis=1, keepdims=True))
    probs = grown / jnp.sum(grown, axis=1, keepdims=True)
    columns = ids.T
    pick = columns[:, 3:4] == iota((t, plan.experts), 1).astype(F32)
    gate = jnp.sum(jnp.where(pick, probs, 0.0), axis=1, keepdims=True)
    aux_out[...] = jnp.where(iota((t, 128), 1) == 0, gate, columns)
    dispatch_to(plan, places or slot_rows(plan, ids), routed, routed_send)


    planes = plan.n // 8
    main_rows = 8 * plan.rows
    plane_rows = main_rows + (32 if plan.folded else 0)
    z = me // 8
    ff = w1.shape[1]
    step = 512

    start_all(plan, me, routed_send, land, send_sem, recv_sem)
    own_copy(plan, me, ct_send, ct_recv, ct_sent.at[0]).wait()

    def keep(number, i):
        rows = len(groups[number]) * plane_rows
        src, dst = ((act, act_out), (gi, gi_out))[i]
        return pltpu.make_async_copy(
            src.at[0:rows, :], dst.at[pl.ds(groups[number][0] * plane_rows, rows), :], out_sem.at[2 * number + i]
        )

    def place_of(kz):
        source = plan.plane_at(z, plan.plane_back(kz))
        return pl.ds(pl.multiple_of(source * main_rows, main_rows), main_rows)

    def assemble(kz, packed, target):
        base = kz * plane_rows
        place = place_of(kz)
        target[base : base + main_rows, :] = packed[place, 0 : plan.width]
        if plan.folded:
            target[base + main_rows : base + plane_rows, :] = unfold(
                packed[place, 768:1024], main_rows
            )

    def pack(kz, values, target):
        place = place_of(kz)
        target[place, 0 : plan.width] = values[0:main_rows, :]
        if plan.folded:
            first, second = refold(plan, values[main_rows:plane_rows, :], main_rows)
            target[place, 768:896] = first.astype(BF)
            target[place, 896:1024] = second.astype(BF)

    for number, members in enumerate(groups):
        group = len(members) * plane_rows
        for kz in members:
            if kz == 0:
                own_copy(plan, me, routed_send, land, send_sem.at[0]).wait()
            def arrived(low, carry, kz=kz):
                block_copy(plan, me, kz * 8 + low, ct_send, ct_recv, ct_sent, ct_come).wait_recv()
                block_copy(plan, me, kz * 8 + low, routed_send, land, send_sem, recv_sem).wait_recv()
                return carry
            lax.fori_loop(1 if kz == 0 else 0, 8, arrived, 0)
            assemble(kz, land, rows_out)
            assemble(kz, ct_recv, gret_out)
        if number == 0:
            def gone(k, carry):
                block_copy(plan, me, k, ct_send, ct_recv, ct_sent, ct_come).wait_send()
                return carry
            lax.fori_loop(1, plan.n, gone, 0)
            loads[4].wait()
            loads[5].wait()
        mine = slice(members[0] * plane_rows, members[0] * plane_rows + group)
        rows = rows_out[mine, :]
        raw = gret_out[mine, :]
        logits = nt(rows, rw_ref[...])
        grown = jnp.exp(logits - jnp.max(logits, axis=1, keepdims=True))
        probs = grown / jnp.sum(grown, axis=1, keepdims=True)
        chosen = jnp.where(iota((group, plan.experts), 1) == me, 1.0, 0.0)
        gate = jnp.sum(probs * chosen, axis=1, keepdims=True)
        gret_out[mine, :] = (gate * raw.astype(F32)).astype(BF)
        if number > 0:
            for i in (0, 1):
                keep(number - 1, i).wait()
        for at in range(0, ff, step):
            cols = slice(at, at + step)
            inner = nn(rows_out[mine, :], w1[:, cols])
            grad = nt(gret_out[mine, :], w2[cols, :])
            square = inner * inner
            slope = 0.7978845608028654 + 0.1070322244 * square
            tanh = jnp.tanh(inner * (0.7978845608028654 + 0.035677408136300125 * square))
            half = 0.5 + 0.5 * tanh
            act[0:group, cols] = (inner * half).astype(BF)
            gi[0:group, cols] = (grad * (half + 0.5 * inner * (1.0 - tanh * tanh) * slope)).astype(BF)
            if at == 0:
                pool[0:group, 0:768] = nn(act[0:group, cols], w2[cols, :])
                pool[group : 2 * group, 0:768] = nt(gi[0:group, cols], w1[:, cols])
            else:
                pool[0:group, 0:768] += nn(act[0:group, cols], w2[cols, :])
                pool[group : 2 * group, 0:768] += nt(gi[0:group, cols], w1[:, cols])
        answer = pool[0:group, 0:768].astype(BF)
        grad_gate = jnp.sum(raw.astype(F32) * answer.astype(F32), axis=1, keepdims=True)
        grad_logits = (probs * (chosen - gate) * grad_gate).astype(BF)
        gl_all[mine, :] = grad_logits
        back = (pool[group : 2 * group, 0:768] + nn(grad_logits, rw_ref[...])).astype(BF)
        for at, kz in enumerate(members):
            part = slice(at * plane_rows, (at + 1) * plane_rows)
            pack(kz, back[part, :], ct_send)
            if kz == 0:
                own_copy(plan, me, ct_send, home_out, back_send.at[0]).start()
            def send(low, carry, kz=kz):
                k = plan.plane_back(kz) * 8 + low
                block_copy(plan, me, k, ct_send, home_out, back_send, back_recv).start()
                return carry
            lax.fori_loop(1 if kz == 0 else 0, 8, send, 0)
            pack(kz, answer[part, :], land)
        for i in (0, 1):
            keep(number, i).start()
    give_back = pltpu.make_async_copy(land, ret_out, save_sem.at[6])
    give_back.start()
    rgrad_out[...] = tn(gl_all[...], rows_out[...])
    for i in (0, 1):
        keep(len(groups) - 1, i).wait()
    for i in range(6):
        save(i).wait()
    give_back.wait()

    def drain(h, carry):
        pltpu.make_async_copy(e_buf.at[h], e_out.at[h], e_sem.at[h]).wait()
        return carry

    lax.fori_loop(0, plan.heads, drain, 0)

    def sent(k, carry):
        block_copy(plan, me, k, routed_send, land, send_sem, recv_sem).wait_send()
        return carry

    lax.fori_loop(1, plan.n, sent, 0)
    wait_all(plan, me, ct_send, home_out, back_send, back_recv)


def forward_part(plan, x, seg, eidx, g1, wq, wk, wv, wo, table, g2, rw, ct, w1, w2):
    planes = plan.n // 8
    groups = ((2,), (0, 1), (3,)) if planes == 4 else tuple((kz,) for kz in range(planes))
    total = plan.slots + plan.extra
    group = max(len(members) for members in groups) * total // planes
    t, w, h, n, e, ff = plan.tokens, plan.width, plan.heads, plan.n, plan.experts, w1.shape[2]
    block = jax.ShapeDtypeStruct((plan.slots, plan.packed), BF)
    state = jax.ShapeDtypeStruct((t, w), BF)
    vmem = pl.BlockSpec(memory_space=pltpu.VMEM)
    any_ = pl.BlockSpec(memory_space=pl.ANY)
    packed = pltpu.VMEM((plan.slots, plan.packed), BF)
    rows = pltpu.VMEM((t, w), BF)
    weight = pltpu.VMEM((w, w), BF)
    each = pltpu.SemaphoreType.DMA((n,))
    return pl.pallas_call(
        functools.partial(forward_kernel, plan, groups),
        out_shape=(
            block,
            jax.ShapeDtypeStruct((h, t, t), BF),
            state, state, state, state, state,
            jax.ShapeDtypeStruct((t, w), F32),
            jax.ShapeDtypeStruct((total, ff), BF),
            jax.ShapeDtypeStruct((total, ff), BF),
            block,
            jax.ShapeDtypeStruct((16, t), F32),
            jax.ShapeDtypeStruct((t, 128), F32),
            jax.ShapeDtypeStruct((total, w), BF),
            jax.ShapeDtypeStruct((total, w), BF),
            jax.ShapeDtypeStruct((e, w), F32),
        ),
        in_specs=[vmem] * 4 + [any_] * 4 + [vmem] * 4 + [any_] * 2,
        out_specs=(any_,) * 11 + (vmem,) * 5,
        scratch_shapes=[
            weight, weight, weight, weight,
            pltpu.VMEM((w, ff), BF),
            pltpu.VMEM((ff, w), BF),
            rows, rows, rows, rows, rows,
            pltpu.VMEM((t, w), F32),
            packed, packed, packed, packed,
            pltpu.VMEM((max(h * 128, 2 * group), SPAN), F32),
            pltpu.VMEM((t, t), F32),
            pltpu.VMEM((t, t), F32),
            pltpu.VMEM((h, t, t), BF),
            pltpu.VMEM((w, t), BF),
            pltpu.VMEM((group, ff), BF),
            pltpu.VMEM((group, ff), BF),
            pltpu.VMEM((total, e), BF),
            each, each, each, each, each, each,
            pltpu.SemaphoreType.DMA((6,)),
            pltpu.SemaphoreType.DMA((7,)),
            pltpu.SemaphoreType.DMA((h,)),
            pltpu.SemaphoreType.DMA((2 * planes,)),
        ],
        compiler_params=pltpu.CompilerParams(
            collective_id=0, has_side_effects=True, vmem_limit_bytes=(60 if n == 32 else 63) * MIB
        ),
        name="forward_and_experts",
    )(x, seg, eidx, g1, wq, wk, wv, wo, table, g2, rw, ct, w1, w2)


class Reducer:
    STEPS = 12

    def __init__(self, plan, me, src, near, wide, slim, far, stages, out, sems, slot):
        self.plan, self.me, self.src, self.out = plan, me, src, out
        self.near, self.wide, self.slim, self.far = near, wide, slim, far
        self.near_stage, self.wide_stage, self.slim_stage = stages
        self.sems, self.slot = sems, slot
        rows = src.shape[0]
        self.half, self.piece, self.own = rows // 2, rows // 16, rows // plan.n
        self.depth = plan.n // 8
        self.core, self.x, self.y, self.z = me % 2, (me // 2) % 2, (me // 4) % 2, me // 8
        self.half_at = self.core * self.half
        self.part_b = self.half_at + self.half // 2

    def span(self, start, size):
        return pl.ds(pl.multiple_of(start, self.own), size)

    def remote(self, src, dst, place, k):
        send, recv = self.sems
        return pltpu.make_async_remote_copy(
            src_ref=src, dst_ref=dst,
            send_sem=send.at[self.slot, place], recv_sem=recv.at[self.slot, place],
            device_id=self.plan.coords(self.plan.peer(self.me, k)), device_id_type=MESH,
        )

    def rows(self, part, x, y, size):
        if part == 0:
            at = self.half_at + (2 * x + (y if size == 1 else 0)) * self.piece
        else:
            at = self.part_b + (2 * y + (x if size == 1 else 0)) * self.piece
        return self.span(at, size * self.piece)

    def owned(self, z):
        late = z // (self.depth // 2)
        a = self.half_at + (2 * self.x + self.y) * self.piece
        b = self.part_b + (2 * self.y + self.x) * self.piece
        return self.span(a + late * (b - a) + (z % (self.depth // 2)) * self.own, self.own)

    def cross(self):
        away = self.span((1 - self.core) * self.half, self.half)
        return [self.remote(self.src.at[away, :], self.near, 0, 1)]

    def first(self):
        return [
            self.remote(self.src.at[self.rows(0, 1 - self.x, self.y, 2), :], self.wide.at[0], 1, 2),
            self.remote(self.src.at[self.rows(1, self.x, 1 - self.y, 2), :], self.wide.at[1], 2, 4),
        ]

    def second(self):
        return [
            self.remote(self.src.at[self.rows(0, self.x, 1 - self.y, 1), :], self.slim.at[0], 3, 4),
            self.remote(self.src.at[self.rows(1, 1 - self.x, self.y, 1), :], self.slim.at[1], 4, 2),
        ]

    def along(self):
        return [
            self.remote(
                self.src.at[self.owned(self.plan.plane_at(self.z, o)), :], self.far.at[o - 1], 9 + o, 8 * o
            )
            for o in range(1, self.depth)
        ]

    def along_back(self):
        place = self.owned(self.z)
        return [
            self.remote(self.src.at[place, :], self.out.at[place, :], 9 + self.depth + o, 8 * o)
            for o in range(1, self.depth)
        ]

    def own_local(self):
        place = self.owned(self.z)
        return pltpu.make_async_copy(
            self.src.at[place, :], self.out.at[place, :], self.sems[0].at[self.slot, 7]
        )

    def again(self, place, sem, k):
        return self.remote(self.out.at[place, :], self.out.at[place, :], sem, k)

    def second_back(self):
        return [self.again(self.rows(0, self.x, self.y, 1), 5, 4), self.again(self.rows(1, self.x, self.y, 1), 6, 2)]

    def first_back(self):
        return [self.again(self.rows(0, self.x, self.y, 2), 8, 2), self.again(self.rows(1, self.x, self.y, 2), 9, 4)]

    def cross_back(self):
        return [self.again(self.span(self.half_at, self.half), 9 + 2 * self.depth, 1)]

    def fetch(self, landed, stage):
        return pltpu.make_async_copy(landed, stage, self.sems[1].at[self.slot, 7])

    def add(self, place, part):
        self.src[place, :] = (self.src[place, :].astype(F32) + part.astype(F32)).astype(BF)

    def step(self, number):
        def start(copies):
            for c in copies:
                c.start()

        def wait(copies):
            for c in copies:
                c.wait()

        if number == 0:
            start(self.cross())
        elif number == 1:
            wait(self.cross())
            self.fetch(self.near, self.near_stage).start()
        elif number == 2:
            self.fetch(self.near, self.near_stage).wait()
            self.add(self.span(self.half_at, self.half), self.near_stage[...])
            start(self.first())
        elif number == 3:
            wait(self.first())
            self.fetch(self.wide, self.wide_stage).start()
        elif number == 4:
            self.fetch(self.wide, self.wide_stage).wait()
            for part in range(2):
                self.add(self.rows(part, self.x, self.y, 2), self.wide_stage[part])
            start(self.second())
        elif number == 5:
            wait(self.second())
            self.fetch(self.slim, self.slim_stage).start()
        elif number == 6:
            self.fetch(self.slim, self.slim_stage).wait()
            for part in range(2):
                self.add(self.rows(part, self.x, self.y, 1), self.slim_stage[part])
            start(self.along())
        elif number == 7:
            wait(self.along())
            place = self.owned(self.z)
            total = self.src[place, :].astype(F32)
            for o in range(self.depth - 1):
                total = total + self.far[o].astype(F32)
            self.src[place, :] = total.astype(BF)
            self.own_local().start()
            start(self.along_back())
        elif number == 8:
            self.own_local().wait()
            wait(self.along_back())
            start(self.second_back())
        elif number == 9:
            wait(self.second_back())
            start(self.first_back())
        elif number == 10:
            wait(self.first_back())
            start(self.cross_back())
        else:
            wait(self.cross_back())


ATTN, TABLE, COUNTS, SMALL = 8, 16, 28, 32


def chunk_rows(plan):
    unit = 16 * plan.n
    square = plan.lanes * plan.width
    return [
        -(-rows // unit) * unit for rows in (square + plan.lanes * plan.experts, square, 4 * plan.width)
    ]


def diagonal_sums(block):
    size = 64
    while size >= 8:
        block = block[0:size, :] + pltpu.roll(block[size : 2 * size, :], SPAN - size, 1)
        size //= 2
    row = iota((8, SPAN), 0)
    for bit in (4, 2, 1):
        block = jnp.where((row // bit) % 2 == 1, pltpu.roll(block, SPAN - bit, 1), block)
    return jnp.sum(block, axis=0, keepdims=True)


def norm_back(values, scale, gain, grad):
    weighted = gain * grad
    inner = jnp.mean(weighted * values, axis=-1, keepdims=True)
    back = scale * weighted - values * (scale * scale * scale * inner)
    return back, jnp.sum(grad * values * scale, axis=0, keepdims=True)


class Small:
    def __init__(self, plan, me, mine, others, send, recv):
        self.plan, self.me, self.mine, self.others, self.send, self.recv = plan, me, mine, others, send, recv

    def copies(self, block, place, offsets, base):
        return [
            pltpu.make_async_remote_copy(
                src_ref=block.at[place], dst_ref=block.at[place],
                send_sem=self.send.at[base + i], recv_sem=self.recv.at[base + i],
                device_id=self.plan.coords(self.plan.peer(self.me, k)), device_id_type=MESH,
            )
            for i, k in enumerate(offsets)
        ]

    def plane(self):
        return self.copies(self.mine, self.me % 8, range(1, 8), 0)

    def along(self):
        return self.copies(self.others, self.me // 8, range(8, self.plan.n, 8), 7)

    def step(self, number):
        if number == 0:
            for c in self.plane():
                c.start()
        elif number == 1:
            for c in self.plane():
                c.wait()
            total = self.mine[0]
            for i in range(1, 8):
                total = total + self.mine[i]
            self.others[self.me // 8] = total
            for c in self.along():
                c.start()
        else:
            for c in self.along():
                c.wait()

    def total(self):
        total = self.others[0]
        for i in range(1, self.plan.n // 8):
            total = total + self.others[i]
        return total


def backward_kernel(
    plan, schedule, batches,
    home_ref, ret_ref, e_hbm, hidden_hbm, ct_hbm, mixed_hbm, wo_hbm, normed_hbm, v_hbm, q_hbm, k_hbm, wq_hbm, wk_hbm,
    wv_hbm, x_hbm, rinv_ref, aux_ref, eidx_ref, g1_ref, g2_ref, rgrad_ref,
    output_out, input_out, flat0_out, flat1_out, flatqk_out, small_out,
    near0_hbm, near1_hbm, nearqk_hbm, mid0_hbm, mid1_hbm, midqk_hbm, slim0_hbm, slim1_hbm, slimqk_hbm,
    hidden_ref, ct_ref, mixed_ref, wo_ref, normed_ref, v_ref, q_ref, k_ref, wq_ref, wk_ref, wv_ref, x_ref,
    home, ret, e_buf, dp_buf, ds_buf, skew, diag, scaled, across, dqt, dq, dk, dv, grad_hidden,
    flat0, flat1, flatqk, near0, near1, nearqk, mid0, mid1, midqk, slim0, slim1, slimqk, far0, far1, farqk, small_plane, small_all,
    send_sem, recv_sem, e_sem, home_sem, load_sem, ar_send, ar_recv, small_send, small_recv,
):
    t, w, e = plan.tokens, plan.width, plan.experts
    me = me_index(plan)
    load_home = pltpu.make_async_copy(home_ref, home, home_sem)
    load_home.start()

    def load_e(h):
        return pltpu.make_async_copy(e_hbm.at[h], e_buf.at[h], e_sem.at[h])

    everyone = greet_all(plan, me)
    HIDDEN, CT, MIXED, WO, NORMED, V, Q, K, WQ, WK, WV, X = range(12)
    loads = [
        pltpu.make_async_copy(src, dst, load_sem.at[i])
        for i, (src, dst) in enumerate(
            ((hidden_hbm, hidden_ref), (ct_hbm, ct_ref), (mixed_hbm, mixed_ref), (wo_hbm, wo_ref),
             (normed_hbm, normed_ref), (v_hbm, v_ref), (q_hbm, q_ref), (k_hbm, k_ref), (wq_hbm, wq_ref),
             (wk_hbm, wk_ref), (wv_hbm, wv_ref), (x_hbm, x_ref))
        )
    ]
    for i in (HIDDEN, CT, MIXED, WO, NORMED):
        loads[i].start()
    for h in range(plan.heads):
        load_e(h).start()
    for i in (V, Q, K, WQ, WK, WV, X):
        loads[i].start()

    sems = (ar_send, ar_recv)
    sums = [
        Reducer(plan, me, flat0, near0_hbm, mid0_hbm, slim0_hbm, far0, (near0, mid0, slim0), flat0_out, sems, 0),
        Reducer(plan, me, flat1, near1_hbm, mid1_hbm, slim1_hbm, far1, (near1, mid1, slim1), flat1_out, sems, 1),
    ] + [
        Reducer(plan, me, flatqk.at[c], nearqk_hbm.at[c], midqk_hbm.at[c], slimqk_hbm.at[c], farqk.at[c],
                (nearqk.at[c], midqk.at[c], slimqk.at[c]), flatqk_out.at[c], sems, 2 + c)
        for c in range(3)
    ]
    sums.append(Small(plan, me, small_plane, small_all, small_send, small_recv))

    def advance(moment):
        for c, number in schedule.get(moment, ()):
            sums[c].step(number)
        if moment in batches:
            first, last = batches[moment]
            first, last = first * plan.n // 32, last * plan.n // 32

            def send(k, carry):
                block_copy(plan, me, k, ret_ref, ret, send_sem, recv_sem).start()
                return carry

            lax.fori_loop(max(first, 1), last, send, 0)
            if first == 0:
                own_copy(plan, me, ret_ref, ret, send_sem.at[0]).start()

    square = plan.lanes * w
    flat0[square + plan.lanes * e :, :] = jnp.zeros((flat0.shape[0] - square - plan.lanes * e, 128), BF)
    if flat1.shape[0] > square:
        flat1[square:, :] = jnp.zeros((flat1.shape[0] - square, 128), BF)
    if flatqk.shape[1] > 4 * w:
        for c in range(3):
            flatqk[c, 4 * w :, :] = jnp.zeros((flatqk.shape[1] - 4 * w, 128), BF)
    for g in range(plan.lanes):
        flat0[square + e * g : square + e * g + e, :] = rgrad_ref[:, 128 * g : 128 * g + 128].astype(BF)

    aux = aux_ref[...]
    gate = aux[:, 0:1]
    dmain = jnp.where(iota((t, plan.slots), 1).astype(F32) == aux[:, 1:2], 1.0, 0.0).astype(BF)
    if plan.folded:
        dextra = jnp.where(iota((t, plan.extra), 1).astype(F32) == aux[:, 2:3], 1.0, 0.0).astype(BF)

    def combine(packed):
        total = nn(dmain, packed[:, 0:w])
        if plan.folded:
            total = total + nn(dextra, unfold(packed[:, 768:1024], plan.slots))
        return total

    def put(target, group, part):
        target[group * w : group * w + w, :] = part[:, 0:128]
        target[group * w + w : group * w + 2 * w, :] = part[:, 128:256]

    loads[MIXED].wait()
    across[...] = mixed_ref[...].T
    everyone()
    advance("early")
    loads[HIDDEN].wait()
    loads[CT].wait()
    load_home.wait()
    hidden = hidden_ref[...]
    back, gain_ffn = norm_back(hidden, rms(hidden), g2_ref[...].reshape(1, w), combine(home))
    grad_hidden[...] = ct_ref[...].astype(F32) + back
    attended = grad_hidden[...].astype(BF)
    for b in range(w // 256):
        put(flat0, 2 * b, nn(across[...], attended[:, 256 * b : 256 * b + 256]).astype(BF))
    advance("out")
    spread = jnp.where(iota((16, w), 1) // plan.head == iota((16, w), 0), 1.0, 0.0)
    shares = jnp.dot(
        rinv_ref[...].T, spread, precision=lax.Precision.HIGHEST, preferred_element_type=F32
    )
    loads[WO].wait()
    loads[NORMED].wait()
    scaled[...] = (nt(attended, wo_ref[...]).astype(BF).astype(F32) * shares).astype(BF)
    across[...] = normed_ref[...].T

    def masked(ref, lanes, side):
        keep = (iota((t, 128), 1) // 64) == side
        return jnp.where(keep, ref[:, lanes], jnp.zeros((), BF))

    for p in range(plan.heads // 2):
        lanes = slice(128 * p, 128 * p + 128)
        load_e(2 * p).wait()
        load_e(2 * p + 1).wait()
        dv[:, lanes] = (
            nn(e_buf[2 * p], masked(scaled, lanes, 0)) + nn(e_buf[2 * p + 1], masked(scaled, lanes, 1))
        ).astype(BF)
    for b in range(w // 256):
        put(flat1, 2 * b, nn(across[...], dv[:, 256 * b : 256 * b + 256]).astype(BF))
    advance("value")
    for i in (V, Q, K):
        loads[i].wait()
    dqt[...] = k_ref[...].T

    for p in range(plan.heads // 2):
        lanes = slice(128 * p, 128 * p + 128)
        dk_pair = jnp.zeros((t, 128), F32)
        for side in range(2):
            h = 2 * p + side
            dom = masked(scaled, lanes, side)
            qm = masked(q_ref, lanes, side)
            skew[h] = jnp.zeros((128, SPAN), F32)
            for ib in range(t // 256):
                cols = slice(256 * ib, 256 * ib + 256)
                delta = jnp.zeros((8, 256), F32)
                for jb in range(t // 128):
                    rows = slice(128 * jb, 128 * jb + 128)
                    dp = nt(v_ref[rows, lanes], dom[cols, :])
                    dp_buf[rows, cols] = dp
                    prod = dp * e_buf[h, rows, cols].astype(F32)
                    delta = delta + jnp.sum(prod.reshape(16, 8, 256), axis=0)
                delta = jnp.sum(delta, axis=0, keepdims=True) * rinv_ref[h : h + 1, cols]
                for jb in range(t // 128):
                    rows = slice(128 * jb, 128 * jb + 128)
                    start = 384 - 128 * jb + 256 * ib
                    ds = e_buf[h, rows, cols].astype(F32) * (dp_buf[rows, cols] - delta)
                    ds_buf[rows, cols] = ds.astype(BF)
                    skew[h, :, start : start + 256] += ds
                advance((h, ib))
            dk_pair = dk_pair + nn(ds_buf[...], qm)
            place = slice(64 * h, 64 * h + 64)
            dqt[place, :] = (nn(dqt[place, :], ds_buf[...]) * score_scale).astype(BF)
            if side == 1:
                dk[:, lanes] = dk_pair.astype(BF)
                dq[:, lanes] = dqt[128 * p : 128 * p + 128, :].T
                if p % 2 == 1:
                    cols = slice(256 * (p // 2), 256 * (p // 2) + 256)
                    target = flatqk.at[p // 2]
                    put(target, 0, nn(across[...], dq[:, cols]).astype(BF))
                    put(target, 2, nn(across[...], dk[:, cols]).astype(BF))
            advance((h, 2))

    advance("first")
    for h in range(plan.heads):
        diag[h : h + 1, :] = diagonal_sums(skew[h])
    for i in (WQ, WK, WV, X):
        loads[i].wait()
    grad_normed = nt(dq[...], wq_ref[...]) + nt(dk[...], wk_ref[...]) + nt(dv[...], wv_ref[...])
    tokens = x_ref[...].astype(F32)
    back, gain_attn = norm_back(tokens, rms(tokens), g1_ref[...].reshape(1, w), grad_normed)
    input_out[...] = (grad_hidden[...] + back).astype(BF)

    small = jnp.zeros((SMALL, 128), F32)
    mine = me % 8
    small_plane[mine] = small
    for g in range(plan.lanes):
        lanes = slice(128 * g, 128 * g + 128)
        small_plane[mine, g : g + 1, :] = gain_ffn[:, lanes]
        small_plane[mine, ATTN + g : ATTN + g + 1, :] = gain_attn[:, lanes]
    sums_table = lax.dot_general(
        diag[0 : plan.heads, :], bucket_onehot(plan.buckets, SPAN), (((1,), (1,)), ((), ())),
        precision=lax.Precision.HIGHEST, preferred_element_type=F32,
    )
    small_plane[mine, TABLE : TABLE + plan.heads, 0 : plan.buckets] = sums_table
    pick = jnp.where(eidx_ref[...] == iota((e, t), 0), 1.0, 0.0).astype(BF)
    load = nt(jnp.ones((8, t), BF), pick)[0:1, :]
    kept = jnp.minimum(load, float(plan.cap))
    small_plane[mine, COUNTS : COUNTS + 1, 0:e] = kept
    small_plane[mine, COUNTS + 1 : COUNTS + 2, 0:e] = load - kept
    advance("second")

    wait_all(plan, me, ret_ref, ret, send_sem, recv_sem)
    output_out[...] = (hidden_ref[...] + gate * combine(ret)).astype(BF)
    advance("third")
    small_out[...] = sums[5].total()


BATCHES = {'early': (16, 32), 'out': (8, 16), 'value': (0, 8)}
SCHEDULE = {
    'out': ((0, 0),),
    'value': ((1, 0),),
    (2, 2): ((0, 1),),
    (3, 2): ((2, 0),),
    (4, 0): ((0, 2), (1, 1)),
    (6, 0): ((1, 2),),
    (6, 1): ((2, 1),),
    (7, 2): ((3, 0), (0, 3), (2, 2)),
    (9, 0): ((0, 4), (1, 3)),
    (10, 2): ((1, 4), (2, 3), (3, 1)),
    (11, 2): ((4, 0), (0, 5), (2, 4), (3, 2)),
    'first': ((1, 5), (0, 6), (1, 6), (2, 5), (4, 1), (2, 6), (4, 2), (3, 3), (0, 7), (3, 4)),
    'second': ((5, 0), (1, 7), (4, 3), (3, 5), (2, 7), (4, 4), (3, 6), (0, 8), (5, 1), (4, 5), (4, 6), (1, 8), (0, 9), (2, 8)),
    'third': ((1, 9), (3, 7), (5, 2), (4, 7), (0, 10), (2, 9), (3, 8), (0, 11), (1, 10), (4, 8), (2, 10), (3, 9), (1, 11), (4, 9), (2, 11), (3, 10), (4, 10), (3, 11), (4, 11)),
}


def backward_part(plan, home, ret, e, rinv, normed, q, k, v, mixed, hidden, aux, eidx, x, ct, wq, wk, wv, wo, g1, g2, rgrad):
    t, w, h, n = plan.tokens, plan.width, plan.heads, plan.n
    r0, r1, rq = chunk_rows(plan)
    depth = n // 8
    places = 10 + 2 * depth
    vmem = pl.BlockSpec(memory_space=pltpu.VMEM)
    any_ = pl.BlockSpec(memory_space=pl.ANY)
    state = jax.ShapeDtypeStruct((t, w), BF)
    bf = lambda *shape: jax.ShapeDtypeStruct(shape, BF)
    rows, weight = pltpu.VMEM((t, w), BF), pltpu.VMEM((w, w), BF)
    return pl.pallas_call(
        functools.partial(backward_kernel, plan, SCHEDULE, BATCHES),
        out_shape=(
            state, state, bf(r0, 128), bf(r1, 128), bf(3, rq, 128),
            jax.ShapeDtypeStruct((SMALL, 128), F32),
            bf(r0 // 2, 128), bf(r1 // 2, 128), bf(3, rq // 2, 128),
            bf(2, r0 // 8, 128), bf(2, r1 // 8, 128), bf(3, 2, rq // 8, 128),
            bf(2, r0 // 16, 128), bf(2, r1 // 16, 128), bf(3, 2, rq // 16, 128),
        ),
        in_specs=[any_] * 15 + [vmem] * 6,
        out_specs=(vmem, vmem, any_, any_, any_, vmem) + (any_,) * 9,
        scratch_shapes=[
            pltpu.VMEM((t, w), F32),
            rows, rows, weight, rows, rows, rows, rows, weight, weight, weight, rows,
            pltpu.VMEM((plan.slots, plan.packed), BF),
            pltpu.VMEM((plan.slots, plan.packed), BF),
            pltpu.VMEM((h, t, t), BF),
            pltpu.VMEM((t, t), F32),
            pltpu.VMEM((t, t), BF),
            pltpu.VMEM((h, 128, SPAN), F32),
            pltpu.VMEM((16, SPAN), F32),
            pltpu.VMEM((t, w), BF),
            pltpu.VMEM((w, t), BF),
            pltpu.VMEM((w, t), BF),
            pltpu.VMEM((t, w), BF),
            pltpu.VMEM((t, w), BF),
            pltpu.VMEM((t, w), BF),
            pltpu.VMEM((t, w), F32),
            pltpu.VMEM((r0, 128), BF),
            pltpu.VMEM((r1, 128), BF),
            pltpu.VMEM((3, rq, 128), BF),
            pltpu.VMEM((r0 // 2, 128), BF),
            pltpu.VMEM((r1 // 2, 128), BF),
            pltpu.VMEM((3, rq // 2, 128), BF),
            pltpu.VMEM((2, r0 // 8, 128), BF),
            pltpu.VMEM((2, r1 // 8, 128), BF),
            pltpu.VMEM((3, 2, rq // 8, 128), BF),
            pltpu.VMEM((2, r0 // 16, 128), BF),
            pltpu.VMEM((2, r1 // 16, 128), BF),
            pltpu.VMEM((3, 2, rq // 16, 128), BF),
            pltpu.VMEM((depth - 1, r0 // n, 128), BF),
            pltpu.VMEM((depth - 1, r1 // n, 128), BF),
            pltpu.VMEM((3, depth - 1, rq // n, 128), BF),
            pltpu.VMEM((8, SMALL, 128), F32),
            pltpu.VMEM((depth, SMALL, 128), F32),
            pltpu.SemaphoreType.DMA((n,)),
            pltpu.SemaphoreType.DMA((n,)),
            pltpu.SemaphoreType.DMA((h,)),
            pltpu.SemaphoreType.DMA,
            pltpu.SemaphoreType.DMA((12,)),
            pltpu.SemaphoreType.DMA((5, places)),
            pltpu.SemaphoreType.DMA((5, places)),
            pltpu.SemaphoreType.DMA((6 + depth,)),
            pltpu.SemaphoreType.DMA((6 + depth,)),
        ],
        compiler_params=pltpu.CompilerParams(
            collective_id=2, has_side_effects=True, vmem_limit_bytes=60 * MIB
        ),
        name="backward_attention",
    )(home, ret, e, hidden, ct, mixed, wo, normed, v, q, k, wq, wk, wv, x, rinv, aux, eidx, g1, g2, rgrad)


def finish_kernel(
    plan, step,
    rows_hbm, gret_hbm, act_hbm, gi_hbm, flat0_hbm, flat1_hbm, flatqk_hbm, output_hbm, input_hbm, small_ref,
    ein_out, eout_out, out_out, v_out, q_out, k_out, output_out, input_out, g1_ref, g2_ref, table_ref, rw_ref, counts_ref,
    rows, gret, act, gi, flat0, flat1, flatqk, turned, ein, eout, square, passing, in_sem, act_sem, gi_sem, ein_sem, eout_sem, out_sem,
):
    w, e = plan.width, plan.experts
    chunks, depth = act_hbm.shape[1] // step, act.shape[0]

    def cut(i):
        return pl.ds(i * step, step)

    load = [
        pltpu.make_async_copy(src, dst, in_sem.at[i])
        for i, (src, dst) in enumerate(
            ((rows_hbm, rows), (gret_hbm, gret), (flat0_hbm, flat0), (flat1_hbm, flat1), (flatqk_hbm, flatqk),
             (output_hbm, passing.at[0]), (input_hbm, passing.at[1]))
        )
    ]
    load_act = [pltpu.make_async_copy(act_hbm.at[:, cut(i)], act.at[i % depth], act_sem.at[i]) for i in range(chunks)]
    load_gi = [pltpu.make_async_copy(gi_hbm.at[:, cut(i)], gi.at[i % depth], gi_sem.at[i]) for i in range(chunks)]
    save_in = [pltpu.make_async_copy(ein.at[:, cut(i)], ein_out.at[0, :, cut(i)], ein_sem.at[i]) for i in range(chunks)]
    save_out = [pltpu.make_async_copy(eout.at[cut(i), :], eout_out.at[0, cut(i), :], eout_sem.at[i]) for i in range(chunks)]
    save = [
        pltpu.make_async_copy(src, dst, out_sem.at[i])
        for i, (src, dst) in enumerate(
            ((square.at[0], out_out), (square.at[1], v_out), (square.at[2], q_out), (square.at[3], k_out),
             (passing.at[0], output_out), (passing.at[1], input_out))
        )
    ]
    for i in (2, 0):
        load[i].start()
    load_gi[0].start()
    load[1].start()
    load_act[0].start()
    for i in (3, 4):
        load[i].start()
    for i in range(1, depth):
        load_gi[i].start()
        load_act[i].start()
    load[5].start()
    load[6].start()

    def lay(m, source, groups):
        for g, at in groups:
            square[m, :, 128 * g : 128 * g + 128] = source(at).astype(F32)
        save[m].start()

    load[2].wait()
    lay(0, lambda at: flat0[at : at + w, :], [(g, g * w) for g in range(plan.lanes)])
    for g in range(plan.lanes):
        lanes = slice(128 * g, 128 * g + 128)
        at = plan.lanes * w + e * g
        rw_ref[:, lanes] = flat0[at : at + e, :].astype(F32)
        g2_ref[lanes] = small_ref[g, :]
        g1_ref[lanes] = small_ref[ATTN + g, :]
    table_ref[...] = small_ref[TABLE : TABLE + plan.heads, 0 : plan.buckets]
    counts_ref[...] = small_ref[COUNTS : COUNTS + 2, 0:e].astype(jnp.int32)
    load[0].wait()
    turned[...] = rows[...].T
    load[1].wait()
    for i in range(chunks):
        cols = slice(i * step, i * step + step)
        load_gi[i].wait()
        ein[:, cols] = nn(turned[...], gi[i % depth])
        save_in[i].start()
        load_act[i].wait()
        eout[cols, :] = tn(act[i % depth], gret[...])
        save_out[i].start()
        if i + depth < chunks:
            load_gi[i + depth].start()
            load_act[i + depth].start()
        if i == 0:
            load[3].wait()
            lay(1, lambda at: flat1[at : at + w, :], [(g, g * w) for g in range(plan.lanes)])
        if i == 1:
            load[4].wait()
            lay(2, lambda at: flatqk[at[0], at[1] : at[1] + w, :], [(g, (g // 2, (g % 2) * w)) for g in range(plan.lanes)])
        if i == 2:
            lay(3, lambda at: flatqk[at[0], at[1] : at[1] + w, :], [(g, (g // 2, (2 + g % 2) * w)) for g in range(plan.lanes)])
    for i in (4, 5):
        load[i + 1].wait()
        save[i].start()
    for copy in save + save_in + save_out:
        copy.wait()


def finish_part(plan, rows, gret, act, gi, flat0, flat1, flatqk, small, output, input_grad):
    t, w, e = plan.tokens, plan.width, plan.experts
    total, ff = act.shape
    step = 512
    chunks = ff // step
    depth = chunks if total <= 1024 else 2
    square = jax.ShapeDtypeStruct((w, w), F32)
    state = jax.ShapeDtypeStruct((t, w), BF)
    vmem = pl.BlockSpec(memory_space=pltpu.VMEM)
    any_ = pl.BlockSpec(memory_space=pl.ANY)
    each = pltpu.SemaphoreType.DMA((chunks,))
    return pl.pallas_call(
        functools.partial(finish_kernel, plan, step),
        out_shape=(
            jax.ShapeDtypeStruct((1, w, ff), F32),
            jax.ShapeDtypeStruct((1, ff, w), F32),
            square, square, square, square, state, state,
            jax.ShapeDtypeStruct((w,), F32),
            jax.ShapeDtypeStruct((w,), F32),
            jax.ShapeDtypeStruct((plan.heads, plan.buckets), F32),
            jax.ShapeDtypeStruct((e, w), F32),
            jax.ShapeDtypeStruct((2, e), jnp.int32),
        ),
        in_specs=[any_] * 9 + [vmem],
        out_specs=(any_,) * 8 + (vmem,) * 5,
        scratch_shapes=[
            pltpu.VMEM((total, w), BF),
            pltpu.VMEM((total, w), BF),
            pltpu.VMEM((depth, total, step), BF),
            pltpu.VMEM((depth, total, step), BF),
            pltpu.VMEM(flat0.shape, BF),
            pltpu.VMEM(flat1.shape, BF),
            pltpu.VMEM(flatqk.shape, BF),
            pltpu.VMEM((w, total), BF),
            pltpu.VMEM((w, ff), F32),
            pltpu.VMEM((ff, w), F32),
            pltpu.VMEM((4, w, w), F32),
            pltpu.VMEM((2, t, w), BF),
            pltpu.SemaphoreType.DMA((7,)),
            each, each, each, each,
            pltpu.SemaphoreType.DMA((6,)),
        ],
        compiler_params=pltpu.CompilerParams(vmem_limit_bytes=60 * MIB),
        name="weight_grads",
    )(rows, gret, act, gi, flat0, flat1, flatqk, output, input_grad, small)


def per_device(
    plan, inputs, segments, expert_index, gain_attn, query_weight, key_weight, value_weight, output_weight,
    bias_table, gain_ffn, router_weight, expert_in, expert_out, cotangent,
):
    eidx = expert_index.reshape(1, plan.tokens)
    g1, g2 = gain_attn, gain_ffn
    router = router_weight.T
    (home, e, normed, q, k, v, mixed, hidden, act, gi, ret, rinv, aux, rows, gret, rgrad) = forward_part(
        plan, inputs, segments, eidx, g1, query_weight, key_weight, value_weight, output_weight,
        bias_table.T, g2, router, cotangent, expert_in, expert_out,
    )
    output, input_grad, flat0, flat1, flatqk, small = backward_part(
        plan, home, ret, e, rinv, normed, q, k, v, mixed, hidden, aux, eidx, inputs, cotangent,
        query_weight, key_weight, value_weight, output_weight, g1, g2, rgrad,
    )[0:6]
    (expert_in_grad, expert_out_grad, out_grad, v_grad, q_grad, k_grad, output, input_grad, gain1, gain2, table,
     router_grad, counts) = finish_part(
        plan, rows, gret, act, gi, flat0, flat1, flatqk, small, output, input_grad
    )
    return (
        output, input_grad, gain1, q_grad, k_grad, v_grad, out_grad, table.T,
        gain2, router_grad.T, expert_in_grad, expert_out_grad, counts,
    )


def solution(mesh):
    split = P(AXES, None)
    cube = P(AXES, None, None)
    n_local = mesh.shape["local"]
    n = mesh.shape["group"] * n_local

    def run(*args):
        tokens, width = args[0].shape
        buckets, heads = args[8].shape
        plan = Plan(n, n_local, tokens, width, args[10].shape[1], heads, buckets)
        return per_device(plan, *args)

    return jax.shard_map(
        run,
        mesh=mesh,
        in_specs=(split, split, split) + (P(),) * 8 + (cube, cube, split),
        out_specs=(split, split) + (P(),) * 8 + (cube, cube, P()),
        check_vma=False,
    )
```
